32 devices in a mesh: gx: 4 (over z), gy: 8 (over y, x, core).
Axes of the slice: x: 2, y: 2, z: 4, core: 2. Of those that a mesh axis runs over, the one named last changes fastest.
Arguments:
- image: float32 [64, 256, 256], P('gx', 'gy'), may hold values from -6 to 6
- phases: int32 [64, 256, 256], P('gx', 'gy'), may hold values from 0 to 2
- phase_table: float32 [2, 3], replicated, may hold values from 0.2 to 8
- start_potential: float32 [64, 256, 256], P('gx', 'gy'), may hold values from 0 to 1
Outputs:
- conductivity: float32 [64, 256, 256], P('gx', 'gy')
- potential: float32 [64, 256, 256], P('gx', 'gy')
The draws below stay inside these ranges and needn't reach their ends.
Inputs may be any that keep to these rules, and one draw needn't show every extreme that they name: `phases`: 0 fibre, 1 binder, 2 pore.
All inputs are finite; a program needn't handle non-finite values.
Results may differ from the reference program's by a relative error of at most 0.00005.
Values sent between devices are 32-bit elements; how exact they have to be, the bound alone decides.
A program may use at most 128 MiB of HBM per device.

```python
import math
import jax
import jax.numpy as jnp

BX = 16
BY = 32
Z = 256
SWEEPS = 3
PHASES = 3
NX = 64
NY = 256


def edge_cells(key, length, brick):
    count = length // brick
    offsets = jax.random.randint(key, (count,), -6, 7)
    edges = jnp.arange(count, dtype=jnp.int32) * brick + offsets.astype(jnp.int32)
    positions = jnp.arange(length, dtype=jnp.int32)
    beyond = (positions[:, None] >= edges[None, 1:]).astype(jnp.int32)
    return jnp.sum(beyond, axis=1).astype(jnp.int32)


def draw_image(key, part):
    keys = jax.random.split(key, 10)
    cell_x = edge_cells(keys[0], NX, BX)
    cell_y = edge_cells(keys[1], NY, BY)
    count_x = NX // BX
    count_y = NY // BY
    loud = jax.random.uniform(keys[2], (count_x, count_y), jnp.float32, 1.7, 2.0)
    quiet = jax.random.uniform(keys[3], (count_x, count_y), jnp.float32, 0.1, 0.4)
    fibre_amp = 3.3
    wave = jax.random.uniform(keys[4], (), jnp.float32, 0.9, 1.1)
    noise = 0.2 * jnp.clip(jax.random.normal(keys[5], (NX, NY, Z), jnp.float32), -3.0, 3.0)
    angle = jax.random.uniform(keys[6], (), jnp.float32, 0.0, math.pi)
    fibre_phase = jax.random.uniform(keys[7], (), jnp.float32, -math.pi, math.pi)
    layer_freq = jax.random.uniform(keys[8], (), jnp.float32, 0.494, 0.5)
    cell_phase = jax.random.uniform(keys[9], (count_x, count_y), jnp.float32, -math.pi, math.pi)
    loud_cells = jnp.take(jnp.take(loud, cell_x, axis=0), cell_y, axis=1)
    quiet_cells = jnp.take(jnp.take(quiet, cell_x, axis=0), cell_y, axis=1)
    phase_cells = jnp.take(jnp.take(cell_phase, cell_x, axis=0), cell_y, axis=1)
    checker = (cell_x[:, None] + cell_y[None, :]) % 2 == 0
    level = jnp.where(checker, loud_cells, quiet_cells)
    pos_x = jnp.arange(NX, dtype=jnp.int32).astype(jnp.float32)
    pos_y = jnp.arange(NY, dtype=jnp.int32).astype(jnp.float32)
    pos_z = jnp.arange(Z, dtype=jnp.int32).astype(jnp.float32)
    fibre = fibre_amp * jnp.sin(wave * (pos_x[:, None] * jnp.cos(angle) + pos_y[None, :] * jnp.sin(angle)) + fibre_phase)
    layers = level[:, :, None] * jnp.sin(layer_freq * pos_z[None, None, :] + phase_cells[:, :, None])
    return (noise + fibre[:, :, None] + layers).astype(jnp.float32)


def draw_phase_table(key, part):
    keys = jax.random.split(key, 2)
    base = jnp.exp(jax.random.uniform(keys[0], (1, PHASES), jnp.float32, math.log(0.2), math.log(2.0)))
    aniso = jnp.exp(jax.random.uniform(keys[1], (1, PHASES), jnp.float32, math.log(4.0), math.log(8.0)))
    return jnp.concatenate([base, aniso], axis=0).astype(jnp.float32)


def with_ends(values, own_key, least, largest):
    extent = values.shape
    place = [jax.random.randint(jax.random.fold_in(own_key, axis), (), 0, extent[axis]) for axis in range(len(extent))]
    values = values.at[tuple(place)].set(least)
    longest = extent.index(max(extent))
    place[longest] = (place[longest] + 1) % extent[longest]
    return values.at[tuple(place)].set(largest)


def shard_levels(key, shape, cuts, least, high):
    def one(position, blocks):
        steps = jax.random.uniform(jax.random.fold_in(jax.random.fold_in(key, 6), position), (blocks,), jnp.float32, least / len(cuts), high / len(cuts))
        return jnp.repeat(jnp.exp(steps), shape[position] // blocks).reshape((-1,) + (1,) * (len(shape) - position - 1))

    gain = one(*cuts[0])
    for cut in cuts[1:]:
        gain = gain * one(*cut)
    return gain


def setup_inputs(seed: int = 0) -> dict:
    streams_of = jax.random.split(jax.random.key(seed), 5)
    return {
        "image": draw_image(jax.random.fold_in(streams_of[4], 71), 0),
        "phases": with_ends(jax.random.randint(streams_of[1], (NX, NY, Z), 0, 3), jax.random.fold_in(streams_of[1], 1), 0, 2).astype(jnp.int32),
        "phase_table": draw_phase_table(jax.random.fold_in(streams_of[4], 71), 0),
        "start_potential": jnp.clip(1.0 * jax.random.uniform(streams_of[3], (NX, NY, Z), jnp.float32) ** shard_levels(streams_of[3], (NX, NY, Z), ((0, 4), (1, 8)), -0.2, 0.2), 0.0, 1.0),
    }


def gauss_taps(sigma, reach, order):
    values = [math.exp(-offset * offset / (2.0 * sigma * sigma)) for offset in range(-reach, reach + 1)]
    total = sum(values)
    values = [value / total for value in values]
    if order == 1:
        values = [(index - reach) * values[index] / (sigma * sigma) for index in range(2 * reach + 1)]
    return values


def filter_dim(field, axis_number, taps):
    reach = (len(taps) - 1) // 2
    widths = [(0, 0), (0, 0), (0, 0)]
    widths[axis_number] = (reach, reach)
    padded = jnp.pad(field, widths)
    length = field.shape[axis_number]
    total = jnp.zeros(field.shape, jnp.float32)
    for offset in range(2 * reach + 1):
        piece = jnp.take(padded, jnp.arange(offset, offset + length, dtype=jnp.int32), axis=axis_number)
        total = total + float(taps[offset]) * piece
    return total


def harmonic(first, second):
    return 2.0 * first * second / (first + second)


def reference(image, phases, phase_table, start_potential):
    near_taps = gauss_taps(1.0, 3, 0)
    slope_taps = gauss_taps(1.0, 3, 1)
    wide_taps = gauss_taps(4.0, 12, 0)
    along = filter_dim(image, 2, near_taps)
    slope = filter_dim(image, 2, slope_taps)
    grad_x = filter_dim(filter_dim(along, 1, near_taps), 0, slope_taps)
    grad_y = filter_dim(filter_dim(along, 1, slope_taps), 0, near_taps)
    grad_z = filter_dim(filter_dim(slope, 1, near_taps), 0, near_taps)

    def smooth(field):
        return filter_dim(filter_dim(filter_dim(field, 2, wide_taps), 1, wide_taps), 0, wide_taps)

    jxx = smooth(grad_x * grad_x)
    jyy = smooth(grad_y * grad_y)
    jzz = smooth(grad_z * grad_z)
    jxy = smooth(grad_x * grad_y)
    jxz = smooth(grad_x * grad_z)
    jyz = smooth(grad_y * grad_z)
    trace = jxx + jyy + jzz
    shift = 0.1 * trace + 1e-6
    first = jxx + shift
    second = jyy + shift
    third = jzz + shift
    cof = first * second - jxy * jxy
    det = first * (second * third - jyz * jyz) - jxy * (jxy * third - jyz * jxz) + jxz * (jxy * jyz - second * jxz)
    weight = trace * cof / det
    conductivity = phase_table[0][phases] + 0.1 * phase_table[1][phases] * weight

    cond_pad = jnp.pad(conductivity, ((1, 1), (1, 1), (0, 0)))
    centre = conductivity
    coef_x0 = harmonic(centre, cond_pad[:-2, 1:-1])
    coef_x1 = harmonic(centre, cond_pad[2:, 1:-1])
    coef_y0 = harmonic(centre, cond_pad[1:-1, :-2])
    coef_y1 = harmonic(centre, cond_pad[1:-1, 2:])
    below = jnp.concatenate([centre[:, :, :1], centre[:, :, :-1]], axis=2)
    above = jnp.concatenate([centre[:, :, 1:], centre[:, :, -1:]], axis=2)
    coef_z0 = harmonic(centre, below)
    coef_z1 = harmonic(centre, above)
    denom = coef_x0 + coef_x1 + coef_y0 + coef_y1 + coef_z0 + coef_z1
    potential = start_potential
    for sweep_index in range(SWEEPS):
        pot_pad = jnp.pad(potential, ((1, 1), (1, 1), (0, 0)))
        pot_below = jnp.concatenate([jnp.ones_like(potential[:, :, :1]), potential[:, :, :-1]], axis=2)
        pot_above = jnp.concatenate([potential[:, :, 1:], jnp.zeros_like(potential[:, :, :1])], axis=2)
        numer = coef_x0 * pot_pad[:-2, 1:-1] + coef_x1 * pot_pad[2:, 1:-1]
        numer = numer + coef_y0 * pot_pad[1:-1, :-2] + coef_y1 * pot_pad[1:-1, 2:]
        numer = numer + coef_z0 * pot_below + coef_z1 * pot_above
        potential = numer / denom
    return conductivity, potential
```

```python
import functools
import math

import jax
import jax.numpy as jnp
import ml_dtypes
import numpy as np
from jax import lax
from jax.experimental import pallas as pl
from jax.experimental.pallas import tpu as pltpu
from jax.sharding import PartitionSpec as P

SWEEPS = 3
PHASES = 3
DERIV = 3
SMOOTH = 12
IMG_X = DERIV + SMOOTH
IMG_Y = 16
POT_X = SWEEPS
POT_Y = 8
MESH = pl.DeviceIdType.MESH
VMEM_LIMIT = 58 * 1024 * 1024
F32 = jnp.float32
BF16 = jnp.bfloat16


def gauss_taps(sigma, reach, order):
    values = [math.exp(-t * t / (2.0 * sigma * sigma)) for t in range(-reach, reach + 1)]
    total = sum(values)
    values = [value / total for value in values]
    if order == 1:
        values = [(i - reach) * values[i] / (sigma * sigma) for i in range(2 * reach + 1)]
    return values


NEAR = gauss_taps(1.0, DERIV, 0)
SLOPE = gauss_taps(1.0, DERIV, 1)
WIDE = gauss_taps(4.0, SMOOTH, 0)


def halves(matrix):
    high = matrix.astype(ml_dtypes.bfloat16)
    low = (matrix - high.astype(np.float32)).astype(ml_dtypes.bfloat16)
    return high, low


def band(out_len, in_len, margin, taps, first=0, last=None):
    reach = (len(taps) - 1) // 2
    matrix = np.zeros((out_len, in_len), np.float32)
    for i in range(first, out_len if last is None else last):
        for t in range(-reach, reach + 1):
            k = i + margin + t
            if 0 <= k < in_len:
                matrix[i, k] = taps[t + reach]
    return matrix


def left_weights(matrix):
    high, low = halves(matrix)
    return np.concatenate([high, high, low], axis=1)


def right_weights(*matrices):
    parts = []
    for matrix in matrices:
        parts += list(halves(np.ascontiguousarray(matrix.T)))
    return np.concatenate(parts, axis=1)


def neighbours():
    gx, gy = lax.axis_index("gx"), lax.axis_index("gy")
    nx, ny = lax.axis_size("gx"), lax.axis_size("gy")
    has_x = (gx > 0, gx < nx - 1)
    has_y = (gy > 0, gy < ny - 1)
    at_x = ((gx - 1, gy), (gx + 1, gy))
    at_y = ((gx, gy - 1), (gx, gy + 1))
    return has_x, has_y, at_x, at_y


def greet():
    has_x, has_y, at_x, at_y = neighbours()
    barrier = pltpu.get_barrier_semaphore()
    for has, at in zip(has_x + has_y, at_x + at_y):
        @pl.when(has)
        def _(at=at):
            pl.semaphore_signal(barrier, inc=1, device_id=at, device_id_type=MESH)
    pl.semaphore_wait(barrier, sum(has.astype(jnp.int32) for has in has_x + has_y))


class Exchange:
    def __init__(self, own, ext, hx, hy, cuts, bands, send, recv, middle=False):
        self.ext, self.hx, self.hy, self.cuts, self.bands = ext, hx, hy, cuts, bands
        self.send, self.recv = send, recv
        self.nx, self.ny = ext.shape[0] - 2 * hx, ext.shape[1] - 2 * hy
        self.own = own
        self.has_x, self.has_y, self.at_x, self.at_y = neighbours()
        gy, half = lax.axis_index("gy"), lax.axis_size("gy") // 2
        if middle:
            self.mid = (gy == half, gy == half - 1)
            self.passes = tuple(
                jnp.logical_and(has, jnp.logical_not(mid))
                for has, mid in zip(self.has_y, self.mid))
        else:
            self.mid, self.passes = None, self.has_y

    @staticmethod
    def count(cuts, bands):
        return 2 * len(bands) + 8 * len(cuts)

    def remote(self, src, dst, index, at):
        return pltpu.make_async_remote_copy(
            src_ref=src, dst_ref=dst, send_sem=self.send.at[index],
            recv_sem=self.recv.at[index], device_id=at, device_id_type=MESH)

    def brick(self, row, rows, col, cols):
        if self.own is None:
            return self.ext.at[pl.ds(self.hx + row, rows), pl.ds(self.hy + col, cols)]
        return self.own.at[pl.ds(row, rows), pl.ds(col, cols)]

    def halo_rows(self, d, cut):
        a, b = cut
        if d == 0:
            return self.nx + self.hx + a, b - a
        return self.hx - b, b - a

    def copy_x(self, d, c):
        a, b = self.cuts[c]
        row, size = self.halo_rows(d, (a, b))
        start = a if d == 0 else self.nx - b
        return self.remote(
            self.brick(start, size, 0, self.ny),
            self.ext.at[pl.ds(row, size), pl.ds(self.hy, self.ny)],
            d * len(self.cuts) + c, self.at_x[d])

    def copy_y(self, d, k):
        a, b = self.bands[k]
        src = 0 if d == 0 else self.ny - self.hy
        dst = self.hy + self.ny if d == 0 else 0
        return self.remote(
            self.brick(a, b - a, src, self.hy),
            self.ext.at[pl.ds(self.hx + a, b - a), pl.ds(dst, self.hy)],
            6 * len(self.cuts) + d * len(self.bands) + k, self.at_y[d])

    def copy_corner(self, side, d, c):
        row, size = self.halo_rows(side, self.cuts[c])
        src = self.hy if d == 0 else self.ny
        dst = self.hy + self.ny if d == 0 else 0
        n = len(self.cuts)
        return self.remote(
            self.ext.at[pl.ds(row, size), pl.ds(src, self.hy)],
            self.ext.at[pl.ds(row, size), pl.ds(dst, self.hy)],
            2 * n + (side * 2 + d) * n + c, self.at_y[d])

    def copy_mid(self, side, d, c):
        a, b = self.cuts[c]
        row, size = self.halo_rows(d, (a, b))
        start = a if d == 0 else self.nx - b
        at = self.hy + self.ny if side == 1 else 0
        return self.remote(
            self.ext.at[pl.ds(self.hx + start, size), pl.ds(at, self.hy)],
            self.ext.at[pl.ds(row, size), pl.ds(at, self.hy)],
            6 * len(self.cuts) + 2 * len(self.bands) + d * len(self.cuts) + c, self.at_x[d])

    def each_mid(self, has, action):
        for side in range(2):
            for d in range(2):
                pl.when(jnp.logical_and(self.mid[side], has[d]))(
                    lambda side=side, d=d: action(side, d))

    def start_mid(self, c):
        self.each_mid(self.has_x, lambda side, d: self.copy_mid(side, d, c).start())

    def wait_mid(self, c):
        self.each_mid(
            self.has_x[::-1], lambda side, d: self.copy_mid(side, d, c).wait_recv())

    def start_x(self, c):
        for d in range(2):
            pl.when(self.has_x[d])(lambda d=d: self.copy_x(d, c).start())

    def start_y(self, k):
        for d in range(2):
            pl.when(self.has_y[d])(lambda d=d: self.copy_y(d, k).start())

    def clear(self):
        rows, cols, z = self.ext.shape
        for d in range(2):
            @pl.when(jnp.logical_not(self.has_x[d]))
            def _(d=d):
                at = 0 if d == 0 else self.hx + self.nx
                self.ext[pl.ds(at, self.hx)] = jnp.zeros((self.hx, cols, z), F32)

            @pl.when(jnp.logical_not(self.has_y[d]))
            def _(d=d):
                at = 0 if d == 0 else self.hy + self.ny
                self.ext[:, pl.ds(at, self.hy)] = jnp.zeros((rows, self.hy, z), F32)

    def forward(self, c):
        for side in range(2):
            @pl.when(self.has_x[1 - side])
            def _(side=side):
                self.copy_x(side, c).wait_recv()
                for d in range(2):
                    pl.when(self.passes[d])(lambda d=d: self.copy_corner(side, d, c).start())

    def wait_y(self, k):
        for d in range(2):
            pl.when(self.has_y[1 - d])(lambda d=d: self.copy_y(d, k).wait_recv())

    def wait_corner(self, c):
        for side in range(2):
            for d in range(2):
                pl.when(jnp.logical_and(self.has_x[1 - side], self.passes[1 - d]))(
                    lambda d=d, side=side: self.copy_corner(side, d, c).wait_recv())
        if self.mid is not None:
            self.wait_mid(c)

    def wait_sends(self):
        for d in range(2):
            for k in range(len(self.bands)):
                pl.when(self.has_y[d])(lambda d=d, k=k: self.copy_y(d, k).wait_send())
            for c in range(len(self.cuts)):
                pl.when(self.has_x[d])(lambda d=d, c=c: self.copy_x(d, c).wait_send())
                for side in range(2):
                    pl.when(jnp.logical_and(self.has_x[1 - side], self.passes[d]))(
                        lambda d=d, c=c, side=side: self.copy_corner(side, d, c).wait_send())
        if self.mid is not None:
            for c in range(len(self.cuts)):
                self.each_mid(
                    self.has_x, lambda side, d, c=c: self.copy_mid(side, d, c).wait_send())


def split(value):
    high = value.astype(BF16)
    return high, (value - high.astype(F32)).astype(BF16)


def dot(a, b):
    return jnp.dot(a, b, preferred_element_type=F32)


def left(weights, value):
    high, low = split(value)
    return dot(weights, jnp.concatenate([high, low, high], axis=0))


def right(value, high_w, low_w):
    high, low = split(value)
    return dot(high, high_w) + dot(low, high_w) + dot(high, low_w)


STEP = 5
IMG_CUTS = tuple((a, a + STEP) for a in range(0, IMG_X, STEP))
POT_CUTS = ((0, POT_X),)


def brick_bands(bx):
    middle = bx // 2
    return ((0, POT_X), (bx - POT_X, bx), (POT_X, middle), (middle, bx - POT_X))


def tensor_kernel(image, phases_in, table_in, start, wg_in, ws_in, zg_in, zs_in, cond, pot,
                  ext, masked, along, smooth, phases, table, wg, ws, zg, zs, *sems):
    gx, gy = lax.axis_index("gx"), lax.axis_index("gy")
    bx, by, z = phases.shape
    size_x, size_y = bx * lax.axis_size("gx"), by * lax.axis_size("gy")
    wide_y = ext.shape[1]
    rows_x = bx + 2 * SMOOTH
    bands = brick_bands(bx)

    img = Exchange(image, ext, IMG_X, IMG_Y, IMG_CUTS, ((0, bx),), *sems[0:2], middle=True)
    pots = Exchange(start, pot, POT_X, POT_Y, POT_CUTS, ((0, bx),), *sems[2:4])
    conds = Exchange(None, cond, POT_X, POT_Y, POT_CUTS, bands, *sems[4:6])
    own_image = pltpu.make_async_copy(
        image, ext.at[pl.ds(IMG_X, bx), pl.ds(IMG_Y, by)], sems[6])
    own_start = pltpu.make_async_copy(
        start, pot.at[pl.ds(POT_X, bx), pl.ds(POT_Y, by)], sems[7])

    loads = [
        pltpu.make_async_copy(src, dst, sems[8 + k])
        for k, (src, dst) in enumerate((
            (wg_in, wg), (zg_in, zg), (ws_in, ws), (phases_in, phases), (zs_in, zs),
            (table_in, table)))
    ]
    own_image.start()
    for load in loads:
        load.start()
    greet()
    img.start_x(0)
    img.start_y(0)
    for c in range(1, len(IMG_CUTS)):
        img.start_x(c)
    own_start.start()
    for part in (img, pots, conds):
        part.clear()

    for load in loads[:3]:
        load.wait()
    row_y = gy * by - IMG_Y + lax.broadcasted_iota(jnp.int32, (wide_y, wg.shape[1]), 0)
    inside = jnp.logical_and(row_y >= 0, row_y < size_y)
    for k in range(2):
        part = wg[k * wide_y:(k + 1) * wide_y].astype(F32)
        masked[k * wide_y:(k + 1) * wide_y] = jnp.where(inside, part, 0.0).astype(BF16)
    own_image.wait()

    def derive(row):
        firsts, seconds = [], []
        for j in range(STEP):
            r = row + j
            at = gx * bx + r - SMOOTH
            ok = jnp.logical_and(at >= 0, at < size_x).astype(F32)
            e = [ext[r + t] for t in range(2 * DERIV + 1)]
            a = e[DERIV] * (NEAR[DERIV] * ok)
            b = jnp.zeros_like(a)
            for t in range(1, DERIV + 1):
                a = a + (e[DERIV + t] + e[DERIV - t]) * (NEAR[DERIV + t] * ok)
                b = b + (e[DERIV + t] - e[DERIV - t]) * (SLOPE[DERIV + t] * ok)
            y_a = left(masked[...], a)
            y_b = left(masked[:wide_y], b)
            firsts += [y_b, y_a[wide_y:]]
            seconds.append(y_a[:wide_y])
        first = right(jnp.concatenate(firsts, axis=0), zg[:, :z], zg[:, z:2 * z])
        second = right(jnp.concatenate(seconds, axis=0), zg[:, 2 * z:3 * z], zg[:, 3 * z:])
        for j in range(STEP):
            r = row + j
            g_x = first[2 * j * wide_y:(2 * j + 1) * wide_y]
            g_y = first[(2 * j + 1) * wide_y:(2 * j + 2) * wide_y]
            g_z = second[j * wide_y:(j + 1) * wide_y]
            for f, (p, q) in enumerate(
                ((g_x, g_x), (g_y, g_y), (g_z, g_z), (g_x, g_y), (g_x, g_z), (g_y, g_z))
            ):
                along[f, r] = left(ws[...], p * q)

    def derive_both(low, high):
        def step(k, carry):
            derive(low + k * (high - low))
            return carry
        lax.fori_loop(0, 2, step, 0)

    centre = rows_x // 2
    img.wait_y(0)
    for c in range(len(IMG_CUTS)):
        img.start_mid(c)
    img.forward(0)
    derive_both(centre - STEP, centre)
    tiles_y, tiles_z = by // 8, z // 128

    def smooth_x(known, ready, add):
        def step(n, carry):
            f = n // (tiles_y * tiles_z)
            ys = pl.ds(pl.multiple_of((n // tiles_z) % tiles_y * 8, 8), 8)
            zz = pl.ds(pl.multiple_of(n % tiles_z * 128, 128), 128)
            new = [r in known and r not in ready for r in range(rows_x)]
            v = [along[f, r, ys, zz] if new[r] else None for r in range(rows_x)]
            for i in range(bx):
                c = i + SMOOTH
                terms = [v[c] * WIDE[SMOOTH]] if new[c] else []
                for t in range(1, SMOOTH + 1):
                    pair = [v[r] for r in (c + t, c - t) if new[r]]
                    if pair:
                        terms.append((pair[0] + pair[1] if len(pair) > 1 else pair[0])
                                     * WIDE[SMOOTH + t])
                if terms:
                    total = smooth[f, i, ys, zz] if add else terms.pop(0)
                    for term in terms:
                        total = total + term
                    smooth[f, i, ys, zz] = total
            return carry
        lax.fori_loop(0, 6 * tiles_y * tiles_z, step, 0)

    last = len(IMG_CUTS) - 1
    for c in range(last):
        img.forward(c + 1)
        img.wait_corner(c)
        derive_both(centre - (c + 2) * STEP, centre + (c + 1) * STEP)
    pots.start_x(0)
    pots.start_y(0)
    inner = range(STEP, rows_x - STEP)
    smooth_x(inner, (), False)
    img.wait_corner(last)
    derive_both(0, rows_x - STEP)
    pots.forward(0)
    smooth_x(range(rows_x), inner, True)
    for load in loads[3:]:
        load.wait()

    def finish(rows):
        every = right(
            jnp.concatenate([smooth[f, i] for i in rows for f in range(6)], axis=0),
            zs[:, :z], zs[:, z:])
        for n, i in enumerate(rows):
            s = every[n * 6 * by:(n + 1) * 6 * by]
            jxx, jyy, jzz, jxy, jxz, jyz = (s[f * by:(f + 1) * by] for f in range(6))
            trace = jxx + jyy + jzz
            shift = 0.1 * trace + 1e-06
            a, b, c = jxx + shift, jyy + shift, jzz + shift
            cof = a * b - jxy * jxy
            det = (
                a * (b * c - jyz * jyz)
                - jxy * (jxy * c - jyz * jxz)
                + jxz * (jxy * jyz - b * jxz)
            )
            weight = trace * cof / det
            label = phases[i]
            base = jnp.where(
                label == 0, table[0, 0], jnp.where(label == 1, table[0, 1], table[0, 2]))
            aniso = jnp.where(
                label == 0, table[1, 0], jnp.where(label == 1, table[1, 1], table[1, 2]))
            cond[POT_X + i, POT_Y:POT_Y + by] = base + 0.1 * aniso * weight

    finish([i for low, high in bands[:2] for i in range(low, high)])
    conds.start_x(0)
    conds.start_y(0)
    conds.start_y(1)
    for k in range(2, len(bands)):
        finish(list(range(*bands[k])))
        conds.start_y(k)
    conds.forward(0)

    own_start.wait()
    pots.wait_y(0)
    pots.wait_corner(0)
    for k in range(len(bands)):
        conds.wait_y(k)
    conds.wait_corner(0)
    for part in (img, pots, conds):
        part.wait_sends()


def tensor(image, phases, table, start):
    bx, by, z = phases.shape
    wide_y = by + 2 * IMG_Y
    rows_x = bx + 2 * SMOOTH
    lo, hi = IMG_Y - SMOOTH, wide_y - (IMG_Y - SMOOTH)
    wg = np.concatenate([
        left_weights(band(wide_y, wide_y, 0, NEAR, lo, hi)),
        left_weights(band(wide_y, wide_y, 0, SLOPE, lo, hi)),
    ], axis=0)
    ws = left_weights(band(by, wide_y, IMG_Y, WIDE))
    zg = right_weights(band(z, z, 0, NEAR), band(z, z, 0, SLOPE))
    zs = right_weights(band(z, z, 0, WIDE))
    vmem = pl.BlockSpec(memory_space=pltpu.VMEM)
    anywhere = pl.BlockSpec(memory_space=pl.ANY)
    outer = jax.ShapeDtypeStruct((bx + 2 * POT_X, by + 2 * POT_Y, z), F32)
    sems = []
    for count in (
        Exchange.count(IMG_CUTS, ((0, bx),)),
        Exchange.count(POT_CUTS, ((0, bx),)),
        Exchange.count(POT_CUTS, brick_bands(bx)),
    ):
        sems += [pltpu.SemaphoreType.DMA((count,))] * 2
    return pl.pallas_call(
        tensor_kernel,
        out_shape=[outer, outer],
        in_specs=[anywhere] * 8,
        out_specs=[vmem, vmem],
        scratch_shapes=[
            pltpu.VMEM((bx + 2 * IMG_X, wide_y, z), F32),
            pltpu.VMEM(wg.shape, BF16),
            pltpu.VMEM((6, rows_x, by, z), F32),
            pltpu.VMEM((6, bx, by, z), F32),
            pltpu.VMEM(phases.shape, jnp.int32),
            pltpu.SMEM(table.shape, F32),
        ] + [pltpu.VMEM(w.shape, BF16) for w in (wg, ws, zg, zs)]
        + sems + [pltpu.SemaphoreType.DMA] * 8,
        compiler_params=pltpu.CompilerParams(
            collective_id=0, has_side_effects=True, vmem_limit_bytes=VMEM_LIMIT),
    )(image, phases, table, start, wg, ws, zg, zs)


def harmonic(p, q):
    total = p + q
    return 2.0 * p * q / jnp.where(total > 0, total, 1.0)


def step_of(count):
    return max(n for n in (1, 2, 3, 4) if count % n == 0)


def sweep_kernel(cond_in, start_in, centre, out, cond, start, kx, y0, y1, z0, z1, inv, one, two,
                 *sems):
    rows, wide, z = cond.shape
    get_cond = pltpu.make_async_copy(cond_in, cond, sems[0])
    get_start = pltpu.make_async_copy(start_in, start, sems[1])
    get_cond.start()
    get_start.start()
    get_cond.wait()
    copy = pltpu.make_async_copy(
        cond.at[pl.ds(POT_X, rows - 2 * POT_X), pl.ds(POT_Y, wide - 2 * POT_Y)], centre, sems[2])
    copy.start()
    lane = lax.broadcasted_iota(jnp.int32, (1, wide, z), 2)
    at_low, at_high = lane == 0, lane == z - 1

    def roll_y(v, s):
        return pltpu.roll(v, s % wide, 1)

    def roll_z(v, s):
        return pltpu.roll(v, s % z, 2)

    kx[0] = harmonic(cond[0], cond[1])
    size = 2

    def coefficients(step, carry):
        j = 1 + step * size
        c = cond[pl.ds(j, size)]
        x_up = harmonic(c, cond[pl.ds(j + 1, size)])
        y_up = harmonic(c, roll_y(c, -1))
        z_up = harmonic(c, roll_z(c, -1))
        x_down = jnp.concatenate([kx[j - 1][None], x_up[:size - 1]], axis=0)
        y_down = roll_y(y_up, 1)
        low = jnp.where(at_low, c, roll_z(z_up, 1))
        high = jnp.where(at_high, c, z_up)
        total = x_down + x_up + y_down + y_up + low + high
        kx[pl.ds(j, size)] = x_up
        y0[pl.ds(j, size)] = y_down
        y1[pl.ds(j, size)] = y_up
        z0[pl.ds(j, size)] = low
        z1[pl.ds(j, size)] = high
        inv[pl.ds(j, size)] = 1.0 / jnp.where(total > 0, total, 1.0)
        return carry

    lax.fori_loop(0, (rows - 2) // size, coefficients, 0)
    get_start.wait()

    def sweep(src, dst, shift, cols, first, last):
        size = step_of(last - first)

        def step(k, carry):
            j = first + k * size
            at = pl.ds(j, size)
            p = src[at]
            numer = kx[pl.ds(j - 1, size)] * src[pl.ds(j - 1, size)]
            numer = numer + kx[at] * src[pl.ds(j + 1, size)]
            numer = numer + y0[at] * roll_y(p, 1) + y1[at] * roll_y(p, -1)
            numer = numer + z0[at] * jnp.where(at_low, 1.0, roll_z(p, 1))
            numer = numer + z1[at] * jnp.where(at_high, 0.0, roll_z(p, -1))
            value = numer * inv[at]
            dst[pl.ds(j - shift, size)] = value[:, cols:wide - cols]
            return carry
        lax.fori_loop(0, (last - first) // size, step, 0)

    sweep(start, one, 0, 0, 1, rows - 1)
    sweep(one, two, 0, 0, 2, rows - 2)
    sweep(two, out, POT_X, POT_Y, 3, rows - 3)
    copy.wait()


def sweeps(cond_ext, pot_ext):
    rows, wide, z = cond_ext.shape
    vmem = pl.BlockSpec(memory_space=pltpu.VMEM)
    brick = jax.ShapeDtypeStruct((rows - 2 * POT_X, wide - 2 * POT_Y, z), F32)
    return pl.pallas_call(
        sweep_kernel,
        out_shape=[brick, brick],
        in_specs=[pl.BlockSpec(memory_space=pl.ANY)] * 2,
        out_specs=[pl.BlockSpec(memory_space=pl.ANY), vmem],
        scratch_shapes=[pltpu.VMEM((rows, wide, z), F32)] * 10 + [pltpu.SemaphoreType.DMA] * 3,
        compiler_params=pltpu.CompilerParams(vmem_limit_bytes=VMEM_LIMIT),
    )(cond_ext, pot_ext)


def body(image, phases, phase_table, start_potential):
    cond_ext, pot_ext = tensor(image, phases, phase_table, start_potential)
    conductivity, potential = sweeps(cond_ext, pot_ext)
    return conductivity, potential


def solution(mesh):
    placed = (P("gx", "gy", None), P("gx", "gy", None), P(), P("gx", "gy", None))
    return jax.shard_map(
        body,
        mesh=mesh,
        in_specs=placed,
        out_specs=(P("gx", "gy", None), P("gx", "gy", None)),
        check_vma=False,
    )
```

```python
import functools
import math

import jax
import jax.numpy as jnp
import ml_dtypes
import numpy as np
from jax import lax
from jax.experimental import pallas as pl
from jax.experimental.pallas import tpu as pltpu
from jax.sharding import PartitionSpec as P

SWEEPS = 3
PHASES = 3
DERIV = 3
SMOOTH = 12
IMG_X = DERIV + SMOOTH
IMG_Y = 16
POT_X = SWEEPS
POT_Y = 8
MESH = pl.DeviceIdType.MESH
VMEM_LIMIT = 32 * 1024 * 1024
F32 = jnp.float32
BF16 = jnp.bfloat16


def gauss_taps(sigma, reach, order):
    values = [math.exp(-t * t / (2.0 * sigma * sigma)) for t in range(-reach, reach + 1)]
    total = sum(values)
    values = [value / total for value in values]
    if order == 1:
        values = [(i - reach) * values[i] / (sigma * sigma) for i in range(2 * reach + 1)]
    return values


NEAR = gauss_taps(1.0, DERIV, 0)
SLOPE = gauss_taps(1.0, DERIV, 1)
WIDE = gauss_taps(4.0, SMOOTH, 0)


def halves(matrix):
    high = matrix.astype(ml_dtypes.bfloat16)
    low = (matrix - high.astype(np.float32)).astype(ml_dtypes.bfloat16)
    return high, low


def band(out_len, in_len, margin, taps, first=0, last=None):
    reach = (len(taps) - 1) // 2
    matrix = np.zeros((out_len, in_len), np.float32)
    for i in range(first, out_len if last is None else last):
        for t in range(-reach, reach + 1):
            k = i + margin + t
            if 0 <= k < in_len:
                matrix[i, k] = taps[t + reach]
    return matrix


def left_weights(matrix):
    high, low = halves(matrix)
    return np.concatenate([high, high, low], axis=1)


def pair_weights(matrix):
    high, low = halves(matrix)
    none = np.zeros_like(high)
    return np.block([
        [high, high, none, none], [low, none, none, none],
        [none, none, high, high], [none, none, low, none]])


def right_weights(*matrices):
    parts = []
    for matrix in matrices:
        parts += list(halves(np.ascontiguousarray(matrix.T)))
    return np.concatenate(parts, axis=1)


def neighbours():
    gx, gy = lax.axis_index("gx"), lax.axis_index("gy")
    nx, ny = lax.axis_size("gx"), lax.axis_size("gy")
    has_x = (gx > 0, gx < nx - 1)
    has_y = (gy > 0, gy < ny - 1)
    at_x = ((gx - 1, gy), (gx + 1, gy))
    at_y = ((gx, gy - 1), (gx, gy + 1))
    return has_x, has_y, at_x, at_y


def greet():
    has_x, has_y, at_x, at_y = neighbours()
    barrier = pltpu.get_barrier_semaphore()
    for has, at in zip(has_x + has_y, at_x + at_y):
        @pl.when(has)
        def _(at=at):
            pl.semaphore_signal(barrier, inc=1, device_id=at, device_id_type=MESH)
    pl.semaphore_wait(barrier, sum(has.astype(jnp.int32) for has in has_x + has_y))


class Exchange:
    def __init__(self, own, ext, hx, hy, cuts, bands, send, recv, middle=False):
        self.ext, self.hx, self.hy, self.cuts, self.bands = ext, hx, hy, cuts, bands
        self.send, self.recv = send, recv
        self.nx, self.ny = ext.shape[0] - 2 * hx, ext.shape[1] - 2 * hy
        self.own = own
        self.has_x, self.has_y, self.at_x, self.at_y = neighbours()
        gy, half = lax.axis_index("gy"), lax.axis_size("gy") // 2
        if middle:
            self.mid = (gy == half, gy == half - 1)
            self.passes = tuple(
                jnp.logical_and(has, jnp.logical_not(mid))
                for has, mid in zip(self.has_y, self.mid))
        else:
            self.mid, self.passes = None, self.has_y

    @staticmethod
    def count(cuts, bands):
        return 2 * len(bands) + 8 * len(cuts)

    def remote(self, src, dst, index, at):
        return pltpu.make_async_remote_copy(
            src_ref=src, dst_ref=dst, send_sem=self.send.at[index],
            recv_sem=self.recv.at[index], device_id=at, device_id_type=MESH)

    def brick(self, row, rows, col, cols):
        if self.own is None:
            return self.ext.at[pl.ds(self.hx + row, rows), pl.ds(self.hy + col, cols)]
        return self.own.at[pl.ds(row, rows), pl.ds(col, cols)]

    def halo_rows(self, d, c):
        size = self.cuts[0][1]
        if d == 0:
            return self.nx + self.hx + c * size, size
        return self.hx - (c + 1) * size, size

    def copy_x(self, d, c):
        row, size = self.halo_rows(d, c)
        start = c * size if d == 0 else self.nx - (c + 1) * size
        return self.remote(
            self.brick(start, size, 0, self.ny),
            self.ext.at[pl.ds(row, size), pl.ds(self.hy, self.ny)],
            d * len(self.cuts) + c, self.at_x[d])

    def copy_y(self, d, k):
        a, b = self.bands[k]
        src = 0 if d == 0 else self.ny - self.hy
        dst = self.hy + self.ny if d == 0 else 0
        return self.remote(
            self.brick(a, b - a, src, self.hy),
            self.ext.at[pl.ds(self.hx + a, b - a), pl.ds(dst, self.hy)],
            6 * len(self.cuts) + d * len(self.bands) + k, self.at_y[d])

    def copy_corner(self, side, d, c):
        row, size = self.halo_rows(side, c)
        src = self.hy if d == 0 else self.ny
        dst = self.hy + self.ny if d == 0 else 0
        n = len(self.cuts)
        return self.remote(
            self.ext.at[pl.ds(row, size), pl.ds(src, self.hy)],
            self.ext.at[pl.ds(row, size), pl.ds(dst, self.hy)],
            2 * n + (side * 2 + d) * n + c, self.at_y[d])

    def copy_mid(self, side, d, c):
        row, size = self.halo_rows(d, c)
        start = c * size if d == 0 else self.nx - (c + 1) * size
        at = self.hy + self.ny if side == 1 else 0
        return self.remote(
            self.ext.at[pl.ds(self.hx + start, size), pl.ds(at, self.hy)],
            self.ext.at[pl.ds(row, size), pl.ds(at, self.hy)],
            6 * len(self.cuts) + 2 * len(self.bands) + d * len(self.cuts) + c, self.at_x[d])

    def each_mid(self, has, action):
        for side in range(2):
            for d in range(2):
                pl.when(jnp.logical_and(self.mid[side], has[d]))(
                    lambda side=side, d=d: action(side, d))

    def start_mid(self, c):
        self.each_mid(self.has_x, lambda side, d: self.copy_mid(side, d, c).start())

    def wait_mid(self, c):
        self.each_mid(
            self.has_x[::-1], lambda side, d: self.copy_mid(side, d, c).wait_recv())

    def start_x(self, c):
        for d in range(2):
            pl.when(self.has_x[d])(lambda d=d: self.copy_x(d, c).start())

    def start_y(self, k):
        for d in range(2):
            pl.when(self.has_y[d])(lambda d=d: self.copy_y(d, k).start())

    def clear(self):
        rows, cols, z = self.ext.shape
        for d in range(2):
            @pl.when(jnp.logical_not(self.has_x[d]))
            def _(d=d):
                at = 0 if d == 0 else self.hx + self.nx
                self.ext[pl.ds(at, self.hx)] = jnp.zeros((self.hx, cols, z), F32)

            @pl.when(jnp.logical_not(self.has_y[d]))
            def _(d=d):
                at = 0 if d == 0 else self.hy + self.ny
                self.ext[:, pl.ds(at, self.hy)] = jnp.zeros((rows, self.hy, z), F32)

    def forward(self, c):
        for side in range(2):
            @pl.when(self.has_x[1 - side])
            def _(side=side):
                self.copy_x(side, c).wait_recv()
                for d in range(2):
                    pl.when(self.passes[d])(lambda d=d: self.copy_corner(side, d, c).start())

    def wait_y(self, k):
        for d in range(2):
            pl.when(self.has_y[1 - d])(lambda d=d: self.copy_y(d, k).wait_recv())

    def wait_corner(self, c):
        for side in range(2):
            for d in range(2):
                pl.when(jnp.logical_and(self.has_x[1 - side], self.passes[1 - d]))(
                    lambda d=d, side=side: self.copy_corner(side, d, c).wait_recv())
        if self.mid is not None:
            self.wait_mid(c)

    def wait_sends(self):
        for d in range(2):
            for k in range(len(self.bands)):
                pl.when(self.has_y[d])(lambda d=d, k=k: self.copy_y(d, k).wait_send())
            for c in range(len(self.cuts)):
                pl.when(self.has_x[d])(lambda d=d, c=c: self.copy_x(d, c).wait_send())
                for side in range(2):
                    pl.when(jnp.logical_and(self.has_x[1 - side], self.passes[d]))(
                        lambda d=d, c=c, side=side: self.copy_corner(side, d, c).wait_send())
        if self.mid is not None:
            for c in range(len(self.cuts)):
                self.each_mid(
                    self.has_x, lambda side, d, c=c: self.copy_mid(side, d, c).wait_send())


def split(value):
    high = value.astype(BF16)
    return high, (value - high.astype(F32)).astype(BF16)


def dot(a, b):
    return jnp.dot(a, b, preferred_element_type=F32)


def left(weights, value):
    high, low = split(value)
    return dot(weights, jnp.concatenate([high, low, high], axis=0))


def right(value, high_w, low_w):
    high, low = split(value)
    return dot(high, high_w) + dot(low, high_w) + dot(high, low_w)


STEP = 5
IMG_CUTS = tuple((a, a + STEP) for a in range(0, IMG_X, STEP))
POT_CUTS = ((0, POT_X),)


def brick_bands(bx):
    return ((0, POT_X), (bx - POT_X, bx), (POT_X, bx - POT_X))


def tensor_kernel(image, phases_in, table_in, start, wg_in, ws_in, zg_in, zs_in, cond, pot,
                  ext, za, zb, grads, masked, along, smooth, phases, table, wg, ws, zg, zs, *sems):
    gx, gy = lax.axis_index("gx"), lax.axis_index("gy")
    bx, by, z = phases.shape
    size_x, size_y = bx * lax.axis_size("gx"), by * lax.axis_size("gy")
    wide_y = ext.shape[1]
    rows_x = bx + 2 * SMOOTH
    bands = brick_bands(bx)

    img = Exchange(image, ext, IMG_X, IMG_Y, IMG_CUTS, ((0, bx),), *sems[0:2], middle=True)
    pots = Exchange(start, pot, POT_X, POT_Y, POT_CUTS, ((0, bx),), *sems[2:4])
    conds = Exchange(None, cond, POT_X, POT_Y, POT_CUTS, bands, *sems[4:6])
    own_image = pltpu.make_async_copy(
        image, ext.at[pl.ds(IMG_X, bx), pl.ds(IMG_Y, by)], sems[6])
    own_start = pltpu.make_async_copy(
        start, pot.at[pl.ds(POT_X, bx), pl.ds(POT_Y, by)], sems[7])

    loads = [
        pltpu.make_async_copy(src, dst, sems[8 + k])
        for k, (src, dst) in enumerate((
            (wg_in, wg), (zg_in, zg), (ws_in, ws), (phases_in, phases), (zs_in, zs),
            (table_in, table)))
    ]
    own_image.start()
    for load in loads:
        load.start()
    greet()
    img.start_x(0)
    img.start_y(0)
    for c in range(1, len(IMG_CUTS)):
        img.start_x(c)
    own_start.start()
    for part in (img, pots, conds):
        part.clear()

    for load in loads[:3]:
        load.wait()
    row_y = gy * by - IMG_Y + lax.broadcasted_iota(jnp.int32, (wide_y, wg.shape[1]), 0)
    inside = jnp.logical_and(row_y >= 0, row_y < size_y)
    for k in range(2):
        part = wg[k * wide_y:(k + 1) * wide_y].astype(F32)
        masked[k * wide_y:(k + 1) * wide_y] = jnp.where(inside, part, 0.0).astype(BF16)
    own_image.wait()

    def along_z(row, rows, col, cols):
        size = rows * cols
        high, low = split(ext[pl.ds(row, rows), pl.ds(col, cols)].reshape(size, z))
        for k, to in enumerate((za, zb)):
            hw, lw = zg[:, 2 * k * z:(2 * k + 1) * z], zg[:, (2 * k + 1) * z:(2 * k + 2) * z]
            out = dot(high, hw) + dot(low, hw) + dot(high, lw)
            to[pl.ds(row, rows), pl.ds(col, cols)] = out.reshape(rows, cols, z)

    def loop(count, action):
        lax.fori_loop(0, count, lambda k, carry: (action(k), carry)[1], 0)

    def gradients(rows, slot):
        for n, r in enumerate(rows):
            at = gx * bx + r - SMOOTH
            ok = jnp.logical_and(at >= 0, at < size_x).astype(F32)
            a = [za[r + t] for t in range(2 * DERIV + 1)]
            b = [zb[r + t] for t in range(2 * DERIV + 1)]
            a_n, b_n = a[DERIV] * (NEAR[DERIV] * ok), b[DERIV] * (NEAR[DERIV] * ok)
            a_s = None
            for t in range(1, DERIV + 1):
                near, slope = NEAR[DERIV + t] * ok, SLOPE[DERIV + t] * ok
                a_n = a_n + (a[DERIV + t] + a[DERIV - t]) * near
                b_n = b_n + (b[DERIV + t] + b[DERIV - t]) * near
                term = (a[DERIV + t] - a[DERIV - t]) * slope
                a_s = term if a_s is None else a_s + term
            grads[slot + 3 * n] = left(masked[:wide_y], a_s)
            grads[slot + 3 * n + 1] = left(masked[wide_y:], a_n)
            grads[slot + 3 * n + 2] = left(masked[:wide_y], b_n)

    def products(rows, slot):
        for n, r in enumerate(rows):
            g = [grads[slot + 3 * n + k] for k in range(3)]
            pairs = ((0, 0), (1, 1), (2, 2), (0, 1), (0, 2), (1, 2))
            for f in range(0, 6, 2):
                parts = []
                for p, q in pairs[f:f + 2]:
                    parts += split(g[p] * g[q])
                out = dot(ws[...], jnp.concatenate(parts, axis=0))
                along[f, r] = out[:by] + out[by:2 * by]
                along[f + 1, r] = out[2 * by:3 * by] + out[3 * by:]

    centre, chunks = rows_x // 2, len(IMG_CUTS)

    def pair_of(k):
        part, j = k // STEP, k % STEP
        return centre - (part + 1) * STEP + j, centre + part * STEP + j

    def derive(part):
        for j in range(STEP + 1):
            if j < STEP:
                gradients(pair_of(part * STEP + j), 6 * j)
            if j > 0:
                products(pair_of(part * STEP + j - 1), 6 * (j - 1))

    tiles_y, tiles_z = by // 8, z // 128

    def smooth_x(known, ready, add):
        def step(n, carry):
            f = n // (tiles_y * tiles_z)
            ys = pl.ds(pl.multiple_of((n // tiles_z) % tiles_y * 8, 8), 8)
            zz = pl.ds(pl.multiple_of(n % tiles_z * 128, 128), 128)
            new = [r in known and r not in ready for r in range(rows_x)]
            v = [along[f, r, ys, zz] if new[r] else None for r in range(rows_x)]
            for i in range(bx):
                c = i + SMOOTH
                terms = [v[c] * WIDE[SMOOTH]] if new[c] else []
                for t in range(1, SMOOTH + 1):
                    pair = [v[r] for r in (c + t, c - t) if new[r]]
                    if pair:
                        terms.append((pair[0] + pair[1] if len(pair) > 1 else pair[0])
                                     * WIDE[SMOOTH + t])
                if terms:
                    total = smooth[f, i, ys, zz] if add else terms.pop(0)
                    for term in terms:
                        total = total + term
                    smooth[f, i, ys, zz] = total
            return carry
        lax.fori_loop(0, 6 * tiles_y * tiles_z, step, 0)

    along_z(IMG_X, bx, IMG_Y, by)
    img.wait_y(0)
    for c in range(chunks):
        img.start_mid(c)
    along_z(IMG_X, bx, 0, IMG_Y)
    along_z(IMG_X, bx, IMG_Y + by, IMG_Y)
    img.forward(0)
    inner = [r for r in range(STEP, rows_x - STEP)]

    def segment(part):
        @pl.when(part == chunks)
        def _():
            pots.start_x(0)
            pots.start_y(0)
            smooth_x(inner, (), False)

        @pl.when(part > 0)
        def _():
            c = part - 1
            pl.when(part < chunks)(lambda: img.forward(c + 1))
            img.wait_corner(c)
            along_z(bx + IMG_X + c * STEP, STEP, 0, wide_y)
            along_z(IMG_X - (c + 1) * STEP, STEP, 0, wide_y)
        derive(part)

    loop(chunks + 1, segment)
    pots.forward(0)
    smooth_x(range(rows_x), inner, True)
    for load in loads[3:]:
        load.wait()

    def along_z_last(rows):
        every = right(
            jnp.concatenate([smooth[f, i] for i in rows for f in range(6)], axis=0),
            zs[:, :z], zs[:, z:])
        grads[:6, :by] = every[:6 * by].reshape(6, by, z)
        grads[:6, by:2 * by] = every[6 * by:].reshape(6, by, z)

    def weigh(rows):
        for n, i in enumerate(rows):
            jxx, jyy, jzz, jxy, jxz, jyz = (grads[f, n * by:(n + 1) * by] for f in range(6))
            trace = jxx + jyy + jzz
            shift = 0.1 * trace + 1e-06
            a, b, c = jxx + shift, jyy + shift, jzz + shift
            cof = a * b - jxy * jxy
            det = (
                a * (b * c - jyz * jyz)
                - jxy * (jxy * c - jyz * jxz)
                + jxz * (jxy * jyz - b * jxz)
            )
            weight = trace * cof / det
            label = phases[i]
            base = jnp.where(
                label == 0, table[0, 0], jnp.where(label == 1, table[0, 1], table[0, 2]))
            aniso = jnp.where(
                label == 0, table[1, 0], jnp.where(label == 1, table[1, 1], table[1, 2]))
            cond[POT_X + i, POT_Y:POT_Y + by] = base + 0.1 * aniso * weight

    def rows_of(k):
        return k, bx - 1 - k

    def finish(k):
        weigh(rows_of(jnp.maximum(k - 1, 0)))
        along_z_last(rows_of(jnp.minimum(k, bx // 2 - 1)))

        @pl.when(k == POT_X)
        def _():
            conds.start_x(0)
            conds.start_y(0)
            conds.start_y(1)

    loop(bx // 2 + 1, finish)
    conds.start_y(2)
    conds.forward(0)

    own_start.wait()
    pots.wait_y(0)
    pots.wait_corner(0)
    for k in range(len(bands)):
        conds.wait_y(k)
    conds.wait_corner(0)
    for part in (img, pots, conds):
        part.wait_sends()


def tensor(image, phases, table, start):
    bx, by, z = phases.shape
    wide_y = by + 2 * IMG_Y
    rows_x = bx + 2 * SMOOTH
    lo, hi = IMG_Y - SMOOTH, wide_y - (IMG_Y - SMOOTH)
    wg = np.concatenate([
        left_weights(band(wide_y, wide_y, 0, NEAR, lo, hi)),
        left_weights(band(wide_y, wide_y, 0, SLOPE, lo, hi)),
    ], axis=0)
    ws = pair_weights(band(by, wide_y, IMG_Y, WIDE))
    zg = right_weights(band(z, z, 0, NEAR), band(z, z, 0, SLOPE))
    zs = right_weights(band(z, z, 0, WIDE))
    vmem = pl.BlockSpec(memory_space=pltpu.VMEM)
    anywhere = pl.BlockSpec(memory_space=pltpu.HBM)
    outer = jax.ShapeDtypeStruct((bx + 2 * POT_X, by + 2 * POT_Y, z), F32)
    sems = []
    for count in (
        Exchange.count(IMG_CUTS, ((0, bx),)),
        Exchange.count(POT_CUTS, ((0, bx),)),
        Exchange.count(POT_CUTS, brick_bands(bx)),
    ):
        sems += [pltpu.SemaphoreType.DMA((count,))] * 2
    return pl.pallas_call(
        tensor_kernel,
        out_shape=[outer, outer],
        in_specs=[anywhere] * 8,
        out_specs=[vmem, vmem],
        scratch_shapes=[
            pltpu.VMEM((bx + 2 * IMG_X, wide_y, z), F32),
            pltpu.VMEM((bx + 2 * IMG_X, wide_y, z), F32),
            pltpu.VMEM((bx + 2 * IMG_X, wide_y, z), F32),
            pltpu.VMEM((6 * STEP, wide_y, z), F32),
            pltpu.VMEM(wg.shape, BF16),
            pltpu.VMEM((6, rows_x, by, z), F32),
            pltpu.VMEM((6, bx, by, z), F32),
            pltpu.VMEM(phases.shape, jnp.int32),
            pltpu.SMEM(table.shape, F32),
        ] + [pltpu.VMEM(w.shape, BF16) for w in (wg, ws, zg, zs)]
        + sems + [pltpu.SemaphoreType.DMA] * 8,
        compiler_params=pltpu.CompilerParams(
            collective_id=0, has_side_effects=True, vmem_limit_bytes=VMEM_LIMIT),
    )(*(pltpu.with_memory_space_constraint(jnp.asarray(x), pltpu.HBM)
        for x in (image, phases, table, start, wg, ws, zg, zs)))


def harmonic(p, q):
    total = p + q
    return 2.0 * p * q / jnp.where(total > 0, total, 1.0)


def step_of(count):
    return max(n for n in (1, 2, 3, 4) if count % n == 0)


def sweep_kernel(cond, start, centre, out, kx, y0, y1, z0, z1, inv, one, two,
                 *sems):
    rows, wide, z = cond.shape
    copy = pltpu.make_async_copy(
        cond.at[pl.ds(POT_X, rows - 2 * POT_X), pl.ds(POT_Y, wide - 2 * POT_Y)], centre, sems[0])
    copy.start()
    lane = lax.broadcasted_iota(jnp.int32, (1, wide, z), 2)
    at_low, at_high = lane == 0, lane == z - 1

    def roll_y(v, s):
        return pltpu.roll(v, s % wide, 1)

    def roll_z(v, s):
        return pltpu.roll(v, s % z, 2)

    kx[0] = harmonic(cond[0], cond[1])
    size = 2

    def coefficients(step, carry):
        j = 1 + step * size
        c = cond[pl.ds(j, size)]
        x_up = harmonic(c, cond[pl.ds(j + 1, size)])
        y_up = harmonic(c, roll_y(c, -1))
        z_up = harmonic(c, roll_z(c, -1))
        x_down = jnp.concatenate([kx[j - 1][None], x_up[:size - 1]], axis=0)
        y_down = roll_y(y_up, 1)
        low = jnp.where(at_low, c, roll_z(z_up, 1))
        high = jnp.where(at_high, c, z_up)
        total = x_down + x_up + y_down + y_up + low + high
        kx[pl.ds(j, size)] = x_up
        y0[pl.ds(j, size)] = y_down
        y1[pl.ds(j, size)] = y_up
        z0[pl.ds(j, size)] = low
        z1[pl.ds(j, size)] = high
        inv[pl.ds(j, size)] = 1.0 / jnp.where(total > 0, total, 1.0)
        return carry

    lax.fori_loop(0, (rows - 2) // size, coefficients, 0)

    def sweep(src, dst, shift, cols, first, last):
        size = step_of(last - first)

        def step(k, carry):
            j = first + k * size
            at = pl.ds(j, size)
            p = src[at]
            numer = kx[pl.ds(j - 1, size)] * src[pl.ds(j - 1, size)]
            numer = numer + kx[at] * src[pl.ds(j + 1, size)]
            numer = numer + y0[at] * roll_y(p, 1) + y1[at] * roll_y(p, -1)
            numer = numer + z0[at] * jnp.where(at_low, 1.0, roll_z(p, 1))
            numer = numer + z1[at] * jnp.where(at_high, 0.0, roll_z(p, -1))
            value = numer * inv[at]
            dst[pl.ds(j - shift, size)] = value[:, cols:wide - cols]
            return carry
        lax.fori_loop(0, (last - first) // size, step, 0)

    sweep(start, one, 0, 0, 1, rows - 1)
    sweep(one, two, 0, 0, 2, rows - 2)
    sweep(two, out, POT_X, POT_Y, 3, rows - 3)
    copy.wait()


def sweeps(cond_ext, pot_ext):
    rows, wide, z = cond_ext.shape
    vmem = pl.BlockSpec(memory_space=pltpu.VMEM)
    brick = jax.ShapeDtypeStruct((rows - 2 * POT_X, wide - 2 * POT_Y, z), F32)
    return pl.pallas_call(
        sweep_kernel,
        out_shape=[brick, brick],
        in_specs=[vmem] * 2,
        out_specs=[pl.BlockSpec(memory_space=pl.ANY), vmem],
        scratch_shapes=[pltpu.VMEM((rows, wide, z), F32)] * 8 + [pltpu.SemaphoreType.DMA],
        compiler_params=pltpu.CompilerParams(vmem_limit_bytes=VMEM_LIMIT),
    )(cond_ext, pot_ext)


def body(image, phases, phase_table, start_potential):
    cond_ext, pot_ext = tensor(image, phases, phase_table, start_potential)
    conductivity, potential = sweeps(cond_ext, pot_ext)
    return conductivity, potential


def solution(mesh):
    placed = (P("gx", "gy", None), P("gx", "gy", None), P(), P("gx", "gy", None))
    return jax.shard_map(
        body,
        mesh=mesh,
        in_specs=placed,
        out_specs=(P("gx", "gy", None), P("gx", "gy", None)),
        check_vma=False,
    )
```

```python
import functools
import math

import jax
import jax.numpy as jnp
import ml_dtypes
import numpy as np
from jax import lax
from jax.experimental import pallas as pl
from jax.experimental.pallas import tpu as pltpu
from jax.sharding import PartitionSpec as P

SWEEPS = 3
PHASES = 3
DERIV = 3
SMOOTH = 12
IMG_X = DERIV + SMOOTH
IMG_Y = 16
POT_X = SWEEPS
POT_Y = 8
MESH = pl.DeviceIdType.MESH
VMEM_LIMIT = 32 * 1024 * 1024
F32 = jnp.float32
BF16 = jnp.bfloat16


def gauss_taps(sigma, reach, order):
    values = [math.exp(-t * t / (2.0 * sigma * sigma)) for t in range(-reach, reach + 1)]
    total = sum(values)
    values = [value / total for value in values]
    if order == 1:
        values = [(i - reach) * values[i] / (sigma * sigma) for i in range(2 * reach + 1)]
    return values


NEAR = gauss_taps(1.0, DERIV, 0)
SLOPE = gauss_taps(1.0, DERIV, 1)
WIDE = gauss_taps(4.0, SMOOTH, 0)


def halves(matrix):
    high = matrix.astype(ml_dtypes.bfloat16)
    low = (matrix - high.astype(np.float32)).astype(ml_dtypes.bfloat16)
    return high, low


def band(out_len, in_len, margin, taps, first=0, last=None):
    reach = (len(taps) - 1) // 2
    matrix = np.zeros((out_len, in_len), np.float32)
    for i in range(first, out_len if last is None else last):
        for t in range(-reach, reach + 1):
            k = i + margin + t
            if 0 <= k < in_len:
                matrix[i, k] = taps[t + reach]
    return matrix


def left_weights(matrix):
    high, low = halves(matrix)
    return np.concatenate([high, high, low], axis=1)


def pair_weights(matrix):
    high, low = halves(matrix)
    none = np.zeros_like(high)
    return np.block([
        [high, high, none, none], [low, none, none, none],
        [none, none, high, high], [none, none, low, none]])


def right_weights(*matrices):
    parts = []
    for matrix in matrices:
        parts += list(halves(np.ascontiguousarray(matrix.T)))
    return np.concatenate(parts, axis=1)


def neighbours():
    gx, gy = lax.axis_index("gx"), lax.axis_index("gy")
    nx, ny = lax.axis_size("gx"), lax.axis_size("gy")
    has_x = (gx > 0, gx < nx - 1)
    has_y = (gy > 0, gy < ny - 1)
    at_x = ((gx - 1, gy), (gx + 1, gy))
    at_y = ((gx, gy - 1), (gx, gy + 1))
    return has_x, has_y, at_x, at_y


def greet():
    has_x, has_y, at_x, at_y = neighbours()
    barrier = pltpu.get_barrier_semaphore()
    known = list(zip(has_x + has_y, at_x + at_y))
    for d in range(2):
        for e in range(2):
            known.append((jnp.logical_and(has_x[d], has_y[e]), (at_x[d][0], at_y[e][1])))
    for has, at in known:
        @pl.when(has)
        def _(at=at):
            pl.semaphore_signal(barrier, inc=1, device_id=at, device_id_type=MESH)
    pl.semaphore_wait(barrier, sum(has.astype(jnp.int32) for has, _ in known))


class Exchange:
    def __init__(self, own, ext, hx, hy, cuts, bands, send, recv, middle=False):
        self.ext, self.hx, self.hy, self.cuts, self.bands = ext, hx, hy, cuts, bands
        self.send, self.recv = send, recv
        self.nx, self.ny = ext.shape[0] - 2 * hx, ext.shape[1] - 2 * hy
        self.own = own
        self.has_x, self.has_y, self.at_x, self.at_y = neighbours()
        gy, half = lax.axis_index("gy"), lax.axis_size("gy") // 2
        if middle:
            self.mid = (gy == half, gy == half - 1)
            self.passes = tuple(
                jnp.logical_and(has, jnp.logical_not(mid))
                for has, mid in zip(self.has_y, self.mid))
        else:
            self.mid, self.passes = None, self.has_y

    @staticmethod
    def count(cuts, bands):
        return 2 * len(bands) + 8 * len(cuts)

    def remote(self, src, dst, index, at):
        return pltpu.make_async_remote_copy(
            src_ref=src, dst_ref=dst, send_sem=self.send.at[index],
            recv_sem=self.recv.at[index], device_id=at, device_id_type=MESH)

    def brick(self, row, rows, col, cols):
        if self.own is None:
            return self.ext.at[pl.ds(self.hx + row, rows), pl.ds(self.hy + col, cols)]
        return self.own.at[pl.ds(row, rows), pl.ds(col, cols)]

    def halo_rows(self, d, c):
        size = self.cuts[0][1]
        if d == 0:
            return self.nx + self.hx + c * size, size
        return self.hx - (c + 1) * size, size

    def copy_x(self, d, c):
        row, size = self.halo_rows(d, c)
        start = c * size if d == 0 else self.nx - (c + 1) * size
        return self.remote(
            self.brick(start, size, 0, self.ny),
            self.ext.at[pl.ds(row, size), pl.ds(self.hy, self.ny)],
            d * len(self.cuts) + c, self.at_x[d])

    def copy_y(self, d, k):
        a, b = self.bands[k]
        src = 0 if d == 0 else self.ny - self.hy
        dst = self.hy + self.ny if d == 0 else 0
        return self.remote(
            self.brick(a, b - a, src, self.hy),
            self.ext.at[pl.ds(self.hx + a, b - a), pl.ds(dst, self.hy)],
            6 * len(self.cuts) + d * len(self.bands) + k, self.at_y[d])

    def copy_corner(self, side, d, c):
        row, size = self.halo_rows(side, c)
        src = self.hy if d == 0 else self.ny
        dst = self.hy + self.ny if d == 0 else 0
        n = len(self.cuts)
        return self.remote(
            self.ext.at[pl.ds(row, size), pl.ds(src, self.hy)],
            self.ext.at[pl.ds(row, size), pl.ds(dst, self.hy)],
            2 * n + (side * 2 + d) * n + c, self.at_y[d])

    def copy_diagonal(self, d, e):
        row, size = self.halo_rows(d, 0)
        return self.remote(
            self.brick(0 if d == 0 else self.nx - size, size,
                       0 if e == 0 else self.ny - self.hy, self.hy),
            self.ext.at[pl.ds(row, size),
                        pl.ds(self.hy + self.ny if e == 0 else 0, self.hy)],
            2 * len(self.cuts) + 2 * d + e, (self.at_x[d][0], self.at_y[e][1]))

    def each_diagonal(self, has_x, has_y, action):
        for d in range(2):
            for e in range(2):
                pl.when(jnp.logical_and(has_x[d], has_y[e]))(
                    lambda d=d, e=e: action(self.copy_diagonal(d, e)))

    def start_diagonal(self):
        self.each_diagonal(self.has_x, self.has_y, lambda copy: copy.start())

    def wait_all(self):
        for d in range(2):
            pl.when(self.has_x[1 - d])(lambda d=d: self.copy_x(d, 0).wait_recv())
        for k in range(len(self.bands)):
            self.wait_y(k)
        self.each_diagonal(
            self.has_x[::-1], self.has_y[::-1], lambda copy: copy.wait_recv())

    def copy_mid(self, side, d, c):
        row, size = self.halo_rows(d, c)
        start = c * size if d == 0 else self.nx - (c + 1) * size
        at = self.hy + self.ny if side == 1 else 0
        return self.remote(
            self.ext.at[pl.ds(self.hx + start, size), pl.ds(at, self.hy)],
            self.ext.at[pl.ds(row, size), pl.ds(at, self.hy)],
            6 * len(self.cuts) + 2 * len(self.bands) + d * len(self.cuts) + c, self.at_x[d])

    def each_mid(self, has, action):
        for side in range(2):
            for d in range(2):
                pl.when(jnp.logical_and(self.mid[side], has[d]))(
                    lambda side=side, d=d: action(side, d))

    def start_mid(self, c):
        self.each_mid(self.has_x, lambda side, d: self.copy_mid(side, d, c).start())

    def wait_mid(self, c):
        self.each_mid(
            self.has_x[::-1], lambda side, d: self.copy_mid(side, d, c).wait_recv())

    def start_x(self, c):
        for d in range(2):
            pl.when(self.has_x[d])(lambda d=d: self.copy_x(d, c).start())

    def sent_x(self, c):
        for d in range(2):
            pl.when(self.has_x[d])(lambda d=d: self.copy_x(d, c).wait_send())

    def start_y(self, k):
        for d in range(2):
            pl.when(self.has_y[d])(lambda d=d: self.copy_y(d, k).start())

    def clear(self):
        rows, cols, z = self.ext.shape
        for d in range(2):
            @pl.when(jnp.logical_not(self.has_x[d]))
            def _(d=d):
                at = 0 if d == 0 else self.hx + self.nx
                self.ext[pl.ds(at, self.hx)] = jnp.zeros((self.hx, cols, z), F32)

            @pl.when(jnp.logical_not(self.has_y[d]))
            def _(d=d):
                at = 0 if d == 0 else self.hy + self.ny
                self.ext[:, pl.ds(at, self.hy)] = jnp.zeros((rows, self.hy, z), F32)

    def forward(self, c):
        for side in range(2):
            @pl.when(self.has_x[1 - side])
            def _(side=side):
                self.copy_x(side, c).wait_recv()
                for d in range(2):
                    pl.when(self.passes[d])(lambda d=d: self.copy_corner(side, d, c).start())

    def wait_y(self, k):
        for d in range(2):
            pl.when(self.has_y[1 - d])(lambda d=d: self.copy_y(d, k).wait_recv())

    def wait_corner(self, c):
        for side in range(2):
            for d in range(2):
                pl.when(jnp.logical_and(self.has_x[1 - side], self.passes[1 - d]))(
                    lambda d=d, side=side: self.copy_corner(side, d, c).wait_recv())
        if self.mid is not None:
            self.wait_mid(c)

    def wait_sends(self):
        for d in range(2):
            for k in range(len(self.bands)):
                pl.when(self.has_y[d])(lambda d=d, k=k: self.copy_y(d, k).wait_send())
        self.sent_x(len(self.cuts) - 1)
        if self.mid is None:
            self.each_diagonal(self.has_x, self.has_y, lambda copy: copy.wait_send())
            return
        for c in range(len(self.cuts)):
            for side in range(2):
                for d in range(2):
                    pl.when(jnp.logical_and(self.has_x[1 - side], self.passes[d]))(
                        lambda d=d, c=c, side=side: self.copy_corner(side, d, c).wait_send())
            self.each_mid(
                self.has_x, lambda side, d, c=c: self.copy_mid(side, d, c).wait_send())


def split(value):
    high = value.astype(BF16)
    return high, (value - high.astype(F32)).astype(BF16)


def dot(a, b):
    return jnp.dot(a, b, preferred_element_type=F32)


def left(weights, value):
    high, low = split(value)
    return dot(weights, jnp.concatenate([high, low, high], axis=0))


def right(value, high_w, low_w):
    high, low = split(value)
    return dot(high, high_w) + dot(low, high_w) + dot(high, low_w)


STEP = 5
BEFORE = 0.5
IMG_CUTS = tuple((a, a + STEP) for a in range(0, IMG_X, STEP))
POT_CUTS = ((0, POT_X),)


def brick_bands(bx):
    low = [0, POT_X, 2 * POT_X]
    bands = []
    for a, b in zip(low, low[1:]):
        bands += [(a, b), (bx - b, bx - a)]
    return tuple(bands) + ((low[-1], bx - low[-1]),)


def tensor_kernel(image, phases_in, table_in, start, wg_in, ws_in, zg_in, zs_in, cond, pot,
                  ext, za, zb, grads, masked, along, smooth, phases, table, wg, ws, zg, zs, *sems):
    gx, gy = lax.axis_index("gx"), lax.axis_index("gy")
    bx, by, z = phases.shape
    size_x, size_y = bx * lax.axis_size("gx"), by * lax.axis_size("gy")
    wide_y = ext.shape[1]
    rows_x = bx + 2 * SMOOTH
    bands = brick_bands(bx)

    img = Exchange(image, ext, IMG_X, IMG_Y, IMG_CUTS, ((0, bx),), *sems[0:2], middle=True)
    pots = Exchange(start, pot, POT_X, POT_Y, POT_CUTS, ((0, bx),), *sems[2:4])
    conds = Exchange(None, cond, POT_X, POT_Y, POT_CUTS, bands, *sems[4:6])
    own_image = pltpu.make_async_copy(
        image, ext.at[pl.ds(IMG_X, bx), pl.ds(IMG_Y, by)], sems[6])
    own_start = pltpu.make_async_copy(
        start, pot.at[pl.ds(POT_X, bx), pl.ds(POT_Y, by)], sems[7])

    loads = [
        pltpu.make_async_copy(src, dst, sems[8 + k])
        for k, (src, dst) in enumerate((
            (wg_in, wg), (zg_in, zg), (ws_in, ws), (phases_in, phases), (zs_in, zs),
            (table_in, table)))
    ]
    own_image.start()
    for load in loads:
        load.start()
    greet()
    img.start_x(0)
    img.start_y(0)
    own_start.start()
    for part in (img, pots, conds):
        part.clear()

    for load in loads[:3]:
        load.wait()
    row_y = gy * by - IMG_Y + lax.broadcasted_iota(jnp.int32, (wide_y, wg.shape[1]), 0)
    inside = jnp.logical_and(row_y >= 0, row_y < size_y)
    for k in range(2):
        part = wg[k * wide_y:(k + 1) * wide_y].astype(F32)
        masked[k * wide_y:(k + 1) * wide_y] = jnp.where(inside, part, 0.0).astype(BF16)
    own_image.wait()

    def along_z(row, rows, col, cols):
        size = rows * cols
        high, low = split(ext[pl.ds(row, rows), pl.ds(col, cols)].reshape(size, z))
        for k, to in enumerate((za, zb)):
            hw, lw = zg[:, 2 * k * z:(2 * k + 1) * z], zg[:, (2 * k + 1) * z:(2 * k + 2) * z]
            out = dot(high, hw) + dot(low, hw) + dot(high, lw)
            to[pl.ds(row, rows), pl.ds(col, cols)] = out.reshape(rows, cols, z)

    def loop(count, action):
        lax.fori_loop(0, count, lambda k, carry: (action(k), carry)[1], 0)

    def gradients(rows, slot):
        for n, r in enumerate(rows):
            at = gx * bx + r - SMOOTH
            ok = jnp.logical_and(at >= 0, at < size_x).astype(F32)
            a = [za[r + t] for t in range(2 * DERIV + 1)]
            b = [zb[r + t] for t in range(2 * DERIV + 1)]
            a_n, b_n = a[DERIV] * (NEAR[DERIV] * ok), b[DERIV] * (NEAR[DERIV] * ok)
            a_s = None
            for t in range(1, DERIV + 1):
                near, slope = NEAR[DERIV + t] * ok, SLOPE[DERIV + t] * ok
                a_n = a_n + (a[DERIV + t] + a[DERIV - t]) * near
                b_n = b_n + (b[DERIV + t] + b[DERIV - t]) * near
                term = (a[DERIV + t] - a[DERIV - t]) * slope
                a_s = term if a_s is None else a_s + term
            grads[slot + 3 * n] = left(masked[:wide_y], a_s)
            grads[slot + 3 * n + 1] = left(masked[wide_y:], a_n)
            grads[slot + 3 * n + 2] = left(masked[:wide_y], b_n)

    def products(rows, slot):
        for n, r in enumerate(rows):
            g = [grads[slot + 3 * n + k] for k in range(3)]
            pairs = ((0, 0), (1, 1), (2, 2), (0, 1), (0, 2), (1, 2))
            for f in range(0, 6, 2):
                parts = []
                for p, q in pairs[f:f + 2]:
                    parts += split(g[p] * g[q])
                out = dot(ws[...], jnp.concatenate(parts, axis=0))
                along[f, r] = out[:by] + out[by:2 * by]
                along[f + 1, r] = out[2 * by:3 * by] + out[3 * by:]

    centre, chunks = rows_x // 2, len(IMG_CUTS)

    def pair_of(k):
        part, j = k // STEP, k % STEP
        return centre - (part + 1) * STEP + j, centre + part * STEP + j

    def derive(part):
        for j in range(STEP + 1):
            if j < STEP:
                gradients(pair_of(part * STEP + j), 6 * j)
            if j > 0:
                products(pair_of(part * STEP + j - 1), 6 * (j - 1))

    tiles_y, tiles_z = by // 8, z // 128

    def smooth_x(known, ready, tiles, first=0, last=1):
        new = [r in known and r not in ready for r in range(rows_x)]

        def tile(n):
            f = n // (tiles_y * tiles_z)
            ys = pl.ds(pl.multiple_of((n // tiles_z) % tiles_y * 8, 8), 8)
            zz = pl.ds(pl.multiple_of(n % tiles_z * 128, 128), 128)
            v = [along[f, r, ys, zz] if new[r] else None for r in range(rows_x)]
            for i in range(bx):
                c = i + SMOOTH
                terms = [v[c] * WIDE[SMOOTH]] if new[c] else []
                for t in range(1, SMOOTH + 1):
                    pair = [v[r] for r in (c + t, c - t) if new[r]]
                    if pair:
                        terms.append((pair[0] + pair[1] if len(pair) > 1 else pair[0])
                                     * WIDE[SMOOTH + t])
                if terms:
                    total = smooth[f, i, ys, zz] if ready else terms.pop(0)
                    for term in terms:
                        total = total + term
                    smooth[f, i, ys, zz] = total

        def step(n):
            for k in range(tiles):
                tile(n * tiles + k)
        count = 6 * tiles_y * tiles_z // tiles
        begin, end = (round(count * part) for part in (first, last))
        lax.fori_loop(begin, end, lambda n, carry: (step(n), carry)[1], 0)

    along_z(IMG_X, bx, IMG_Y, by)
    img.sent_x(0)
    img.start_x(1)
    img.wait_y(0)
    img.start_mid(0)
    img.forward(0)
    along_z(IMG_X, bx, 0, IMG_Y)
    along_z(IMG_X, bx, IMG_Y + by, IMG_Y)
    img.sent_x(1)
    img.start_x(2)
    img.start_mid(1)
    img.start_mid(2)
    core = range((chunks - 1) * STEP, rows_x - (chunks - 1) * STEP)
    inner = range(STEP, rows_x - STEP)

    def segment(part):
        @pl.when(part == chunks)
        def _():
            pots.start_y(0)
            pots.start_diagonal()
            smooth_x(inner, core, 4)

        @pl.when(part > 0)
        def _():
            c = part - 1
            pl.when(part == chunks - 1)(lambda: smooth_x(core, (), 2, 0, BEFORE))
            pl.when(part < chunks)(lambda: img.forward(c + 1))

            @pl.when(part == chunks - 1)
            def _():
                pots.start_x(0)
                smooth_x(core, (), 2, BEFORE, 1)
            img.wait_corner(c)
            along_z(bx + IMG_X + c * STEP, STEP, 0, wide_y)
            along_z(IMG_X - (c + 1) * STEP, STEP, 0, wide_y)
        derive(part)

    loop(chunks + 1, segment)
    smooth_x(range(rows_x), inner, 4)
    for load in loads[3:]:
        load.wait()

    def along_z_last(rows, slot):
        every = right(
            jnp.concatenate([smooth[f, i] for i in rows for f in range(6)], axis=0),
            zs[:, :z], zs[:, z:])
        grads[slot:slot + 6, :by] = every[:6 * by].reshape(6, by, z)
        grads[slot:slot + 6, by:2 * by] = every[6 * by:].reshape(6, by, z)

    def weigh(rows, slot):
        for n, i in enumerate(rows):
            jxx, jyy, jzz, jxy, jxz, jyz = (
                grads[slot + f, n * by:(n + 1) * by] for f in range(6))
            trace = jxx + jyy + jzz
            shift = 0.1 * trace + 1e-06
            a, b, c = jxx + shift, jyy + shift, jzz + shift
            cof = a * b - jxy * jxy
            det = (
                a * (b * c - jyz * jyz)
                - jxy * (jxy * c - jyz * jxz)
                + jxz * (jxy * jyz - b * jxz)
            )
            weight = trace * cof / det
            label = phases[i]
            base = jnp.where(
                label == 0, table[0, 0], jnp.where(label == 1, table[0, 1], table[0, 2]))
            aniso = jnp.where(
                label == 0, table[1, 0], jnp.where(label == 1, table[1, 1], table[1, 2]))
            cond[POT_X + i, POT_Y:POT_Y + by] = base + 0.1 * aniso * weight

    def rows_of(k):
        return k, bx - 1 - k

    pairs = bx // 2
    for k in range(pairs + 1):
        if k < pairs:
            along_z_last(rows_of(k), 6 * (k % STEP))
        if k > 0:
            weigh(rows_of(k - 1), 6 * ((k - 1) % STEP))
        if k == POT_X:
            conds.start_x(0)
            conds.start_diagonal()
            conds.start_y(0)
            conds.start_y(1)
        if k == 2 * POT_X:
            conds.start_y(2)
            conds.start_y(3)
    conds.start_y(4)

    own_start.wait()
    pots.wait_all()
    conds.wait_all()
    for part in (img, pots, conds):
        part.wait_sends()


def tensor(image, phases, table, start):
    bx, by, z = phases.shape
    wide_y = by + 2 * IMG_Y
    rows_x = bx + 2 * SMOOTH
    lo, hi = IMG_Y - SMOOTH, wide_y - (IMG_Y - SMOOTH)
    wg = np.concatenate([
        left_weights(band(wide_y, wide_y, 0, NEAR, lo, hi)),
        left_weights(band(wide_y, wide_y, 0, SLOPE, lo, hi)),
    ], axis=0)
    ws = pair_weights(band(by, wide_y, IMG_Y, WIDE))
    zg = right_weights(band(z, z, 0, NEAR), band(z, z, 0, SLOPE))
    zs = right_weights(band(z, z, 0, WIDE))
    vmem = pl.BlockSpec(memory_space=pltpu.VMEM)
    anywhere = pl.BlockSpec(memory_space=pltpu.HBM)
    outer = jax.ShapeDtypeStruct((bx + 2 * POT_X, by + 2 * POT_Y, z), F32)
    sems = []
    for count in (
        Exchange.count(IMG_CUTS, ((0, bx),)),
        Exchange.count(POT_CUTS, ((0, bx),)),
        Exchange.count(POT_CUTS, brick_bands(bx)),
    ):
        sems += [pltpu.SemaphoreType.DMA((count,))] * 2
    return pl.pallas_call(
        tensor_kernel,
        out_shape=[outer, outer],
        in_specs=[anywhere] * 8,
        out_specs=[vmem, vmem],
        scratch_shapes=[
            pltpu.VMEM((bx + 2 * IMG_X, wide_y, z), F32),
            pltpu.VMEM((bx + 2 * IMG_X, wide_y, z), F32),
            pltpu.VMEM((bx + 2 * IMG_X, wide_y, z), F32),
            pltpu.VMEM((6 * STEP, wide_y, z), F32),
            pltpu.VMEM(wg.shape, BF16),
            pltpu.VMEM((6, rows_x, by, z), F32),
            pltpu.VMEM((6, bx, by, z), F32),
            pltpu.VMEM(phases.shape, jnp.int32),
            pltpu.SMEM(table.shape, F32),
        ] + [pltpu.VMEM(w.shape, BF16) for w in (wg, ws, zg, zs)]
        + sems + [pltpu.SemaphoreType.DMA] * 8,
        compiler_params=pltpu.CompilerParams(
            collective_id=0, has_side_effects=True, vmem_limit_bytes=VMEM_LIMIT),
    )(*(pltpu.with_memory_space_constraint(jnp.asarray(x), pltpu.HBM)
        for x in (image, phases, table, start, wg, ws, zg, zs)))


def harmonic(p, q):
    total = p + q
    return 2.0 * p * q / jnp.where(total > 0, total, 1.0)


def step_of(count):
    return max(n for n in (1, 2, 3, 4) if count % n == 0)


def sweep_kernel(cond, start, centre, out, kx, y0, y1, z0, z1, inv, one, two,
                 *sems):
    rows, wide, z = cond.shape
    copy = pltpu.make_async_copy(
        cond.at[pl.ds(POT_X, rows - 2 * POT_X), pl.ds(POT_Y, wide - 2 * POT_Y)], centre, sems[0])
    copy.start()
    lane = lax.broadcasted_iota(jnp.int32, (1, wide, z), 2)
    at_low, at_high = lane == 0, lane == z - 1

    def roll_y(v, s):
        return pltpu.roll(v, s % wide, 1)

    def roll_z(v, s):
        return pltpu.roll(v, s % z, 2)

    kx[0] = harmonic(cond[0], cond[1])
    size = 2

    def coefficients(step, carry):
        j = 1 + step * size
        c = cond[pl.ds(j, size)]
        x_up = harmonic(c, cond[pl.ds(j + 1, size)])
        y_up = harmonic(c, roll_y(c, -1))
        z_up = harmonic(c, roll_z(c, -1))
        x_down = jnp.concatenate([kx[j - 1][None], x_up[:size - 1]], axis=0)
        y_down = roll_y(y_up, 1)
        low = jnp.where(at_low, c, roll_z(z_up, 1))
        high = jnp.where(at_high, c, z_up)
        total = x_down + x_up + y_down + y_up + low + high
        kx[pl.ds(j, size)] = x_up
        y0[pl.ds(j, size)] = y_down
        y1[pl.ds(j, size)] = y_up
        z0[pl.ds(j, size)] = low
        z1[pl.ds(j, size)] = high
        inv[pl.ds(j, size)] = 1.0 / jnp.where(total > 0, total, 1.0)
        return carry

    lax.fori_loop(0, (rows - 2) // size, coefficients, 0)

    def sweep(src, dst, shift, cols, first, last):
        size = step_of(last - first)

        def step(k, carry):
            j = first + k * size
            at = pl.ds(j, size)
            p = src[at]
            numer = kx[pl.ds(j - 1, size)] * src[pl.ds(j - 1, size)]
            numer = numer + kx[at] * src[pl.ds(j + 1, size)]
            numer = numer + y0[at] * roll_y(p, 1) + y1[at] * roll_y(p, -1)
            numer = numer + z0[at] * jnp.where(at_low, 1.0, roll_z(p, 1))
            numer = numer + z1[at] * jnp.where(at_high, 0.0, roll_z(p, -1))
            value = numer * inv[at]
            dst[pl.ds(j - shift, size)] = value[:, cols:wide - cols]
            return carry
        lax.fori_loop(0, (last - first) // size, step, 0)

    sweep(start, one, 0, 0, 1, rows - 1)
    sweep(one, two, 0, 0, 2, rows - 2)
    sweep(two, out, POT_X, POT_Y, 3, rows - 3)
    copy.wait()


def sweeps(cond_ext, pot_ext):
    rows, wide, z = cond_ext.shape
    vmem = pl.BlockSpec(memory_space=pltpu.VMEM)
    brick = jax.ShapeDtypeStruct((rows - 2 * POT_X, wide - 2 * POT_Y, z), F32)
    return pl.pallas_call(
        sweep_kernel,
        out_shape=[brick, brick],
        in_specs=[vmem] * 2,
        out_specs=[pl.BlockSpec(memory_space=pl.ANY), vmem],
        scratch_shapes=[pltpu.VMEM((rows, wide, z), F32)] * 8 + [pltpu.SemaphoreType.DMA],
        compiler_params=pltpu.CompilerParams(vmem_limit_bytes=VMEM_LIMIT),
    )(cond_ext, pot_ext)


def body(image, phases, phase_table, start_potential):
    cond_ext, pot_ext = tensor(image, phases, phase_table, start_potential)
    conductivity, potential = sweeps(cond_ext, pot_ext)
    return conductivity, potential


def solution(mesh):
    placed = (P("gx", "gy", None), P("gx", "gy", None), P(), P("gx", "gy", None))
    return jax.shard_map(
        body,
        mesh=mesh,
        in_specs=placed,
        out_specs=(P("gx", "gy", None), P("gx", "gy", None)),
        check_vma=False,
    )
```

```python
import functools
import math

import jax
import jax.numpy as jnp
import ml_dtypes
import numpy as np
from jax import lax
from jax.experimental import pallas as pl
from jax.experimental.pallas import tpu as pltpu
from jax.sharding import PartitionSpec as P

SWEEPS = 3
PHASES = 3
DERIV = 3
SMOOTH = 12
IMG_X = DERIV + SMOOTH
IMG_Y = 16
POT_X = SWEEPS
POT_Y = 8
MESH = pl.DeviceIdType.MESH
VMEM_LIMIT = 32 * 1024 * 1024
F32 = jnp.float32
BF16 = jnp.bfloat16


def gauss_taps(sigma, reach, order):
    values = [math.exp(-t * t / (2.0 * sigma * sigma)) for t in range(-reach, reach + 1)]
    total = sum(values)
    values = [value / total for value in values]
    if order == 1:
        values = [(i - reach) * values[i] / (sigma * sigma) for i in range(2 * reach + 1)]
    return values


NEAR = gauss_taps(1.0, DERIV, 0)
SLOPE = gauss_taps(1.0, DERIV, 1)
WIDE = gauss_taps(4.0, SMOOTH, 0)


def halves(matrix):
    high = matrix.astype(ml_dtypes.bfloat16)
    low = (matrix - high.astype(np.float32)).astype(ml_dtypes.bfloat16)
    return high, low


def band(out_len, in_len, margin, taps, first=0, last=None):
    reach = (len(taps) - 1) // 2
    matrix = np.zeros((out_len, in_len), np.float32)
    for i in range(first, out_len if last is None else last):
        for t in range(-reach, reach + 1):
            k = i + margin + t
            if 0 <= k < in_len:
                matrix[i, k] = taps[t + reach]
    return matrix


def left_weights(matrix):
    high, low = halves(matrix)
    return np.concatenate([high, high, low], axis=1)


def pair_weights(matrix):
    high, low = halves(matrix)
    none = np.zeros_like(high)
    return np.block([
        [high, high, none, none], [low, none, none, none],
        [none, none, high, high], [none, none, low, none]])


def right_weights(*matrices):
    parts = []
    for matrix in matrices:
        parts += list(halves(np.ascontiguousarray(matrix.T)))
    return np.concatenate(parts, axis=1)


def neighbours():
    gx, gy = lax.axis_index("gx"), lax.axis_index("gy")
    nx, ny = lax.axis_size("gx"), lax.axis_size("gy")
    has_x = (gx > 0, gx < nx - 1)
    has_y = (gy > 0, gy < ny - 1)
    at_x = ((gx - 1, gy), (gx + 1, gy))
    at_y = ((gx, gy - 1), (gx, gy + 1))
    return has_x, has_y, at_x, at_y


def greet():
    has_x, has_y, at_x, at_y = neighbours()
    barrier = pltpu.get_barrier_semaphore()
    known = list(zip(has_x + has_y, at_x + at_y))
    for d in range(2):
        for e in range(2):
            known.append((jnp.logical_and(has_x[d], has_y[e]), (at_x[d][0], at_y[e][1])))
    for has, at in known:
        @pl.when(has)
        def _(at=at):
            pl.semaphore_signal(barrier, inc=1, device_id=at, device_id_type=MESH)
    pl.semaphore_wait(barrier, sum(has.astype(jnp.int32) for has, _ in known))


class Exchange:
    def __init__(self, own, ext, hx, hy, cuts, bands, send, recv, middle=False):
        self.ext, self.hx, self.hy, self.cuts, self.bands = ext, hx, hy, cuts, bands
        self.send, self.recv = send, recv
        self.nx, self.ny = ext.shape[0] - 2 * hx, ext.shape[1] - 2 * hy
        self.own = own
        self.has_x, self.has_y, self.at_x, self.at_y = neighbours()
        gy, half = lax.axis_index("gy"), lax.axis_size("gy") // 2
        if middle:
            self.mid = (gy == half, gy == half - 1)
            self.passes = tuple(
                jnp.logical_and(has, jnp.logical_not(mid))
                for has, mid in zip(self.has_y, self.mid))
        else:
            self.mid, self.passes = None, self.has_y

    @staticmethod
    def count(cuts, bands):
        return 2 * len(bands) + 10 * len(cuts)

    def remote(self, src, dst, index, at):
        return pltpu.make_async_remote_copy(
            src_ref=src, dst_ref=dst, send_sem=self.send.at[index],
            recv_sem=self.recv.at[index], device_id=at, device_id_type=MESH)

    def brick(self, row, rows, col, cols):
        if self.own is None:
            return self.ext.at[pl.ds(self.hx + row, rows), pl.ds(self.hy + col, cols)]
        return self.own.at[pl.ds(row, rows), pl.ds(col, cols)]

    def halo_rows(self, d, c):
        size = self.cuts[0][1]
        if d == 0:
            return self.nx + self.hx + c * size, size
        return self.hx - (c + 1) * size, size

    def copy_x(self, d, c, half=None):
        row, size = self.halo_rows(d, c)
        start = c * size if d == 0 else self.nx - (c + 1) * size
        n = len(self.cuts)
        if half is None:
            col, cols, index = 0, self.ny, d * n + c
        else:
            col, cols = half * (self.ny // 2), self.ny // 2
            index = (d if half == 0 else 8 + d) * n + half * 2 * len(self.bands) + c
        return self.remote(
            self.brick(start, size, col, cols),
            self.ext.at[pl.ds(row, size), pl.ds(self.hy + col, cols)],
            index, self.at_x[d])

    def copy_y(self, d, k):
        a, b = self.bands[k]
        src = 0 if d == 0 else self.ny - self.hy
        dst = self.hy + self.ny if d == 0 else 0
        return self.remote(
            self.brick(a, b - a, src, self.hy),
            self.ext.at[pl.ds(self.hx + a, b - a), pl.ds(dst, self.hy)],
            6 * len(self.cuts) + d * len(self.bands) + k, self.at_y[d])

    def copy_corner(self, side, d, c):
        row, size = self.halo_rows(side, c)
        src = self.hy if d == 0 else self.ny
        dst = self.hy + self.ny if d == 0 else 0
        n = len(self.cuts)
        return self.remote(
            self.ext.at[pl.ds(row, size), pl.ds(src, self.hy)],
            self.ext.at[pl.ds(row, size), pl.ds(dst, self.hy)],
            2 * n + (side * 2 + d) * n + c, self.at_y[d])

    def copy_diagonal(self, d, e):
        row, size = self.halo_rows(d, 0)
        return self.remote(
            self.brick(0 if d == 0 else self.nx - size, size,
                       0 if e == 0 else self.ny - self.hy, self.hy),
            self.ext.at[pl.ds(row, size),
                        pl.ds(self.hy + self.ny if e == 0 else 0, self.hy)],
            2 * len(self.cuts) + 2 * d + e, (self.at_x[d][0], self.at_y[e][1]))

    def each_diagonal(self, has_x, has_y, action):
        for d in range(2):
            for e in range(2):
                pl.when(jnp.logical_and(has_x[d], has_y[e]))(
                    lambda d=d, e=e: action(self.copy_diagonal(d, e)))

    def start_diagonal(self):
        self.each_diagonal(self.has_x, self.has_y, lambda copy: copy.start())

    def wait_all(self):
        for d in range(2):
            pl.when(self.has_x[1 - d])(lambda d=d: self.copy_x(d, 0).wait_recv())
        for k in range(len(self.bands)):
            self.wait_y(k)
        self.each_diagonal(
            self.has_x[::-1], self.has_y[::-1], lambda copy: copy.wait_recv())

    def copy_mid(self, side, d, c):
        row, size = self.halo_rows(d, c)
        start = c * size if d == 0 else self.nx - (c + 1) * size
        at = self.hy + self.ny if side == 1 else 0
        return self.remote(
            self.ext.at[pl.ds(self.hx + start, size), pl.ds(at, self.hy)],
            self.ext.at[pl.ds(row, size), pl.ds(at, self.hy)],
            6 * len(self.cuts) + 2 * len(self.bands) + d * len(self.cuts) + c, self.at_x[d])

    def each_mid(self, has, action):
        for side in range(2):
            for d in range(2):
                pl.when(jnp.logical_and(self.mid[side], has[d]))(
                    lambda side=side, d=d: action(side, d))

    def start_mid(self, c):
        self.each_mid(self.has_x, lambda side, d: self.copy_mid(side, d, c).start())

    def wait_mid(self, c):
        self.each_mid(
            self.has_x[::-1], lambda side, d: self.copy_mid(side, d, c).wait_recv())

    def start_x(self, c, half=None):
        for d in range(2):
            pl.when(self.has_x[d])(lambda d=d: self.copy_x(d, c, half).start())

    def sent_x(self, c, half=None):
        for d in range(2):
            pl.when(self.has_x[d])(lambda d=d: self.copy_x(d, c, half).wait_send())

    def start_y(self, k):
        for d in range(2):
            pl.when(self.has_y[d])(lambda d=d: self.copy_y(d, k).start())

    def clear(self):
        rows, cols, z = self.ext.shape
        for d in range(2):
            @pl.when(jnp.logical_not(self.has_x[d]))
            def _(d=d):
                at = 0 if d == 0 else self.hx + self.nx
                self.ext[pl.ds(at, self.hx)] = jnp.zeros((self.hx, cols, z), F32)

            @pl.when(jnp.logical_not(self.has_y[d]))
            def _(d=d):
                at = 0 if d == 0 else self.hy + self.ny
                self.ext[:, pl.ds(at, self.hy)] = jnp.zeros((rows, self.hy, z), F32)

    def forward(self, c):
        for d in range(2):
            for side in range(2):
                @pl.when(self.has_x[1 - side])
                def _(side=side, d=d):
                    self.copy_x(side, c, d).wait_recv()
                    pl.when(self.passes[d])(lambda: self.copy_corner(side, d, c).start())

    def wait_y(self, k):
        for d in range(2):
            pl.when(self.has_y[1 - d])(lambda d=d: self.copy_y(d, k).wait_recv())

    def wait_corner(self, c):
        for side in range(2):
            for d in range(2):
                pl.when(jnp.logical_and(self.has_x[1 - side], self.passes[1 - d]))(
                    lambda d=d, side=side: self.copy_corner(side, d, c).wait_recv())
        if self.mid is not None:
            self.wait_mid(c)

    def wait_sends(self):
        for d in range(2):
            for k in range(len(self.bands)):
                pl.when(self.has_y[d])(lambda d=d, k=k: self.copy_y(d, k).wait_send())
        if self.mid is None:
            self.sent_x(0)
            self.each_diagonal(self.has_x, self.has_y, lambda copy: copy.wait_send())
            return
        for half in range(2):
            self.sent_x(len(self.cuts) - 1, half)
        for c in range(len(self.cuts)):
            for side in range(2):
                for d in range(2):
                    pl.when(jnp.logical_and(self.has_x[1 - side], self.passes[d]))(
                        lambda d=d, c=c, side=side: self.copy_corner(side, d, c).wait_send())
            self.each_mid(
                self.has_x, lambda side, d, c=c: self.copy_mid(side, d, c).wait_send())


def split(value):
    high = value.astype(BF16)
    return high, (value - high.astype(F32)).astype(BF16)


def dot(a, b):
    return jnp.dot(a, b, preferred_element_type=F32)


def left(weights, value):
    high, low = split(value)
    return dot(weights, jnp.concatenate([high, low, high], axis=0))


def right(value, high_w, low_w):
    high, low = split(value)
    return dot(high, high_w) + dot(low, high_w) + dot(high, low_w)


STEP = 5
IMG_CUTS = tuple((a, a + STEP) for a in range(0, IMG_X, STEP))
POT_CUTS = ((0, POT_X),)


def brick_bands(bx):
    return ((0, POT_X), (bx - POT_X, bx), (POT_X, bx - POT_X))


def tensor_kernel(image, phases_in, table_in, start, wg_in, ws_in, zg_in, zs_in, cond, pot,
                  ext, za, zb, grads, masked, along, smooth, phases, table, wg, ws, zg, zs, *sems):
    gx, gy = lax.axis_index("gx"), lax.axis_index("gy")
    bx, by, z = phases.shape
    size_x, size_y = bx * lax.axis_size("gx"), by * lax.axis_size("gy")
    wide_y = ext.shape[1]
    rows_x = bx + 2 * SMOOTH
    bands = brick_bands(bx)

    img = Exchange(image, ext, IMG_X, IMG_Y, IMG_CUTS, ((0, bx),), *sems[0:2], middle=True)
    pots = Exchange(start, pot, POT_X, POT_Y, POT_CUTS, ((0, bx),), *sems[2:4])
    conds = Exchange(None, cond, POT_X, POT_Y, POT_CUTS, bands, *sems[4:6])
    own_image = pltpu.make_async_copy(
        image, ext.at[pl.ds(IMG_X, bx), pl.ds(IMG_Y, by)], sems[6])
    own_start = pltpu.make_async_copy(
        start, pot.at[pl.ds(POT_X, bx), pl.ds(POT_Y, by)], sems[7])

    loads = [
        pltpu.make_async_copy(src, dst, sems[8 + k])
        for k, (src, dst) in enumerate((
            (wg_in, wg), (zg_in, zg), (ws_in, ws), (phases_in, phases), (zs_in, zs),
            (table_in, table)))
    ]
    own_image.start()
    for load in loads:
        load.start()
    greet()
    img.start_x(0, 0)
    img.start_y(0)
    img.start_x(0, 1)
    own_start.start()
    for part in (img, pots, conds):
        part.clear()

    for load in loads[:3]:
        load.wait()
    row_y = gy * by - IMG_Y + lax.broadcasted_iota(jnp.int32, (wide_y, wg.shape[1]), 0)
    inside = jnp.logical_and(row_y >= 0, row_y < size_y)
    for k in range(2):
        part = wg[k * wide_y:(k + 1) * wide_y].astype(F32)
        masked[k * wide_y:(k + 1) * wide_y] = jnp.where(inside, part, 0.0).astype(BF16)
    own_image.wait()

    def along_z(row, rows, col, cols):
        size = rows * cols
        high, low = split(ext[pl.ds(row, rows), pl.ds(col, cols)].reshape(size, z))
        for k, to in enumerate((za, zb)):
            hw, lw = zg[:, 2 * k * z:(2 * k + 1) * z], zg[:, (2 * k + 1) * z:(2 * k + 2) * z]
            out = dot(high, hw) + dot(low, hw) + dot(high, lw)
            to[pl.ds(row, rows), pl.ds(col, cols)] = out.reshape(rows, cols, z)

    def loop(count, action):
        lax.fori_loop(0, count, lambda k, carry: (action(k), carry)[1], 0)

    def gradients(rows, slot):
        for n, r in enumerate(rows):
            at = gx * bx + r - SMOOTH
            ok = jnp.logical_and(at >= 0, at < size_x).astype(F32)
            a = [za[r + t] for t in range(2 * DERIV + 1)]
            b = [zb[r + t] for t in range(2 * DERIV + 1)]
            a_n, b_n = a[DERIV] * (NEAR[DERIV] * ok), b[DERIV] * (NEAR[DERIV] * ok)
            a_s = None
            for t in range(1, DERIV + 1):
                near, slope = NEAR[DERIV + t] * ok, SLOPE[DERIV + t] * ok
                a_n = a_n + (a[DERIV + t] + a[DERIV - t]) * near
                b_n = b_n + (b[DERIV + t] + b[DERIV - t]) * near
                term = (a[DERIV + t] - a[DERIV - t]) * slope
                a_s = term if a_s is None else a_s + term
            grads[slot + 3 * n] = left(masked[:wide_y], a_s)
            grads[slot + 3 * n + 1] = left(masked[wide_y:], a_n)
            grads[slot + 3 * n + 2] = left(masked[:wide_y], b_n)

    def products(rows, slot):
        for n, r in enumerate(rows):
            g = [grads[slot + 3 * n + k] for k in range(3)]
            pairs = ((0, 0), (1, 1), (2, 2), (0, 1), (0, 2), (1, 2))
            for f in range(0, 6, 2):
                parts = []
                for p, q in pairs[f:f + 2]:
                    parts += split(g[p] * g[q])
                out = dot(ws[...], jnp.concatenate(parts, axis=0))
                along[f, r] = out[:by] + out[by:2 * by]
                along[f + 1, r] = out[2 * by:3 * by] + out[3 * by:]

    centre, chunks = rows_x // 2, len(IMG_CUTS)

    def pair_of(k):
        part, j = k // STEP, k % STEP
        return centre - (part + 1) * STEP + j, centre + part * STEP + j

    def derive(part):
        for j in range(STEP + 1):
            if j < STEP:
                gradients(pair_of(part * STEP + j), 6 * j)
            if j > 0:
                products(pair_of(part * STEP + j - 1), 6 * (j - 1))

    tiles_y, tiles_z = by // 8, z // 128

    def smooth_x(known, ready, tiles):
        new = [r in known and r not in ready for r in range(rows_x)]

        def tile(n):
            f = n // (tiles_y * tiles_z)
            ys = pl.ds(pl.multiple_of((n // tiles_z) % tiles_y * 8, 8), 8)
            zz = pl.ds(pl.multiple_of(n % tiles_z * 128, 128), 128)
            v = [along[f, r, ys, zz] if new[r] else None for r in range(rows_x)]
            for i in range(bx):
                c = i + SMOOTH
                terms = [v[c] * WIDE[SMOOTH]] if new[c] else []
                for t in range(1, SMOOTH + 1):
                    pair = [v[r] for r in (c + t, c - t) if new[r]]
                    if pair:
                        terms.append((pair[0] + pair[1] if len(pair) > 1 else pair[0])
                                     * WIDE[SMOOTH + t])
                if terms:
                    total = smooth[f, i, ys, zz] if ready else terms.pop(0)
                    for term in terms:
                        total = total + term
                    smooth[f, i, ys, zz] = total

        def step(n):
            for k in range(tiles):
                tile(n * tiles + k)
        loop(6 * tiles_y * tiles_z // tiles, step)

    along_z(IMG_X, bx, IMG_Y, by)
    img.sent_x(0, 0)
    img.start_x(1, 0)
    img.sent_x(0, 1)
    img.start_x(1, 1)
    img.wait_y(0)
    img.start_mid(0)
    img.forward(0)
    img.sent_x(1, 0)
    img.start_x(2, 0)
    along_z(IMG_X, bx, 0, IMG_Y)
    along_z(IMG_X, bx, IMG_Y + by, IMG_Y)
    img.start_mid(1)
    img.sent_x(1, 1)
    img.start_x(2, 1)
    img.start_mid(2)
    core = range(chunks * STEP, rows_x - chunks * STEP)
    inner = range(STEP, rows_x - STEP)

    def segment(part):
        @pl.when(part == chunks)
        def _():
            pots.start_y(0)
            pots.start_diagonal()
            smooth_x(inner, core, 4)

        @pl.when(part > 0)
        def _():
            c = part - 1
            pl.when(part == 1)(lambda: smooth_x(core, (), 4))
            pl.when(part < chunks)(lambda: img.forward(c + 1))

            @pl.when(part == chunks - 1)
            def _():
                pots.start_x(0)
            img.wait_corner(c)
            along_z(bx + IMG_X + c * STEP, STEP, 0, wide_y)
            along_z(IMG_X - (c + 1) * STEP, STEP, 0, wide_y)
        derive(part)

    loop(chunks + 1, segment)
    smooth_x(range(rows_x), inner, 4)
    for load in loads[3:]:
        load.wait()

    def along_z_last(parts, slot):
        every = right(
            jnp.concatenate([smooth[f, i, a:b] for i, a, b in parts for f in range(6)], axis=0),
            zs[:, :z], zs[:, z:])
        at = 0
        for n, (i, a, b) in enumerate(parts):
            for f in range(6):
                grads[slot + f, n * 16:n * 16 + b - a] = every[at:at + b - a]
                at += b - a

    def weigh(parts, slot):
        for n, (i, a, b) in enumerate(parts):
            jxx, jyy, jzz, jxy, jxz, jyz = (
                grads[slot + f, n * 16:n * 16 + b - a] for f in range(6))
            trace = jxx + jyy + jzz
            shift = 0.1 * trace + 1e-06
            p, q, c = jxx + shift, jyy + shift, jzz + shift
            cof = p * q - jxy * jxy
            det = (
                p * (q * c - jyz * jyz)
                - jxy * (jxy * c - jyz * jxz)
                + jxz * (jxy * jyz - q * jxz)
            )
            weight = trace * cof / det
            label = phases[i, a:b]
            base = jnp.where(
                label == 0, table[0, 0], jnp.where(label == 1, table[0, 1], table[0, 2]))
            aniso = jnp.where(
                label == 0, table[1, 0], jnp.where(label == 1, table[1, 1], table[1, 2]))
            cond[POT_X + i, POT_Y + a:POT_Y + b] = base + 0.1 * aniso * weight

    outer = list(range(POT_X)) + list(range(bx - POT_X, bx))
    rest = range(POT_X, bx - POT_X)
    half = by // 2
    units = [[(i, 0, half), (i, half, by)] for i in outer]
    units = [units[k] + units[k + 1] for k in range(0, len(units), 2)]
    first = len(units)
    edges = [[(i, 0, POT_Y), (i, by - POT_Y, by)] for i in rest]
    units += [edges[k] + edges[k + 1] for k in range(0, len(edges), 2)]
    second = len(units)
    middle = [[(i, POT_Y, by - POT_Y)] for i in rest]
    units += [middle[k] + middle[k + 1] for k in range(0, len(middle), 2)]
    for k in range(len(units) + 1):
        if k < len(units):
            along_z_last(units[k], 6 * (k % STEP))
        if k > 0:
            weigh(units[k - 1], 6 * ((k - 1) % STEP))
        if k == first:
            conds.start_x(0)
            conds.start_diagonal()
            conds.start_y(0)
            conds.start_y(1)
        if k == second:
            conds.start_y(2)


    own_start.wait()
    pots.wait_all()
    conds.wait_all()
    for part in (img, pots, conds):
        part.wait_sends()


def tensor(image, phases, table, start):
    bx, by, z = phases.shape
    wide_y = by + 2 * IMG_Y
    rows_x = bx + 2 * SMOOTH
    lo, hi = IMG_Y - SMOOTH, wide_y - (IMG_Y - SMOOTH)
    wg = np.concatenate([
        left_weights(band(wide_y, wide_y, 0, NEAR, lo, hi)),
        left_weights(band(wide_y, wide_y, 0, SLOPE, lo, hi)),
    ], axis=0)
    ws = pair_weights(band(by, wide_y, IMG_Y, WIDE))
    zg = right_weights(band(z, z, 0, NEAR), band(z, z, 0, SLOPE))
    zs = right_weights(band(z, z, 0, WIDE))
    vmem = pl.BlockSpec(memory_space=pltpu.VMEM)
    anywhere = pl.BlockSpec(memory_space=pltpu.HBM)
    outer = jax.ShapeDtypeStruct((bx + 2 * POT_X, by + 2 * POT_Y, z), F32)
    sems = []
    for count in (
        Exchange.count(IMG_CUTS, ((0, bx),)),
        Exchange.count(POT_CUTS, ((0, bx),)),
        Exchange.count(POT_CUTS, brick_bands(bx)),
    ):
        sems += [pltpu.SemaphoreType.DMA((count,))] * 2
    return pl.pallas_call(
        tensor_kernel,
        out_shape=[outer, outer],
        in_specs=[anywhere] * 8,
        out_specs=[vmem, vmem],
        scratch_shapes=[
            pltpu.VMEM((bx + 2 * IMG_X, wide_y, z), F32),
            pltpu.VMEM((bx + 2 * IMG_X, wide_y, z), F32),
            pltpu.VMEM((bx + 2 * IMG_X, wide_y, z), F32),
            pltpu.VMEM((6 * STEP, wide_y, z), F32),
            pltpu.VMEM(wg.shape, BF16),
            pltpu.VMEM((6, rows_x, by, z), F32),
            pltpu.VMEM((6, bx, by, z), F32),
            pltpu.VMEM(phases.shape, jnp.int32),
            pltpu.SMEM(table.shape, F32),
        ] + [pltpu.VMEM(w.shape, BF16) for w in (wg, ws, zg, zs)]
        + sems + [pltpu.SemaphoreType.DMA] * 8,
        compiler_params=pltpu.CompilerParams(
            collective_id=0, has_side_effects=True, vmem_limit_bytes=VMEM_LIMIT),
    )(*(pltpu.with_memory_space_constraint(jnp.asarray(x), pltpu.HBM)
        for x in (image, phases, table, start, wg, ws, zg, zs)))


def harmonic(p, q):
    total = p + q
    return 2.0 * p * q / jnp.where(total > 0, total, 1.0)


def step_of(count):
    return max(n for n in (1, 2, 3, 4) if count % n == 0)


def sweep_kernel(cond, start, centre, out, kx, y0, y1, z0, z1, inv, one, two,
                 *sems):
    rows, wide, z = cond.shape
    copy = pltpu.make_async_copy(
        cond.at[pl.ds(POT_X, rows - 2 * POT_X), pl.ds(POT_Y, wide - 2 * POT_Y)], centre, sems[0])
    copy.start()
    lane = lax.broadcasted_iota(jnp.int32, (1, wide, z), 2)
    at_low, at_high = lane == 0, lane == z - 1

    def roll_y(v, s):
        return pltpu.roll(v, s % wide, 1)

    def roll_z(v, s):
        return pltpu.roll(v, s % z, 2)

    kx[0] = harmonic(cond[0], cond[1])
    size = 2

    def coefficients(step, carry):
        j = 1 + step * size
        c = cond[pl.ds(j, size)]
        x_up = harmonic(c, cond[pl.ds(j + 1, size)])
        y_up = harmonic(c, roll_y(c, -1))
        z_up = harmonic(c, roll_z(c, -1))
        x_down = jnp.concatenate([kx[j - 1][None], x_up[:size - 1]], axis=0)
        y_down = roll_y(y_up, 1)
        low = jnp.where(at_low, c, roll_z(z_up, 1))
        high = jnp.where(at_high, c, z_up)
        total = x_down + x_up + y_down + y_up + low + high
        kx[pl.ds(j, size)] = x_up
        y0[pl.ds(j, size)] = y_down
        y1[pl.ds(j, size)] = y_up
        z0[pl.ds(j, size)] = low
        z1[pl.ds(j, size)] = high
        inv[pl.ds(j, size)] = 1.0 / jnp.where(total > 0, total, 1.0)
        return carry

    lax.fori_loop(0, (rows - 2) // size, coefficients, 0)

    def sweep(src, dst, shift, cols, first, last):
        size = step_of(last - first)

        def step(k, carry):
            j = first + k * size
            at = pl.ds(j, size)
            p = src[at]
            numer = kx[pl.ds(j - 1, size)] * src[pl.ds(j - 1, size)]
            numer = numer + kx[at] * src[pl.ds(j + 1, size)]
            numer = numer + y0[at] * roll_y(p, 1) + y1[at] * roll_y(p, -1)
            numer = numer + z0[at] * jnp.where(at_low, 1.0, roll_z(p, 1))
            numer = numer + z1[at] * jnp.where(at_high, 0.0, roll_z(p, -1))
            value = numer * inv[at]
            dst[pl.ds(j - shift, size)] = value[:, cols:wide - cols]
            return carry
        lax.fori_loop(0, (last - first) // size, step, 0)

    sweep(start, one, 0, 0, 1, rows - 1)
    sweep(one, two, 0, 0, 2, rows - 2)
    sweep(two, out, POT_X, POT_Y, 3, rows - 3)
    copy.wait()


def sweeps(cond_ext, pot_ext):
    rows, wide, z = cond_ext.shape
    vmem = pl.BlockSpec(memory_space=pltpu.VMEM)
    brick = jax.ShapeDtypeStruct((rows - 2 * POT_X, wide - 2 * POT_Y, z), F32)
    return pl.pallas_call(
        sweep_kernel,
        out_shape=[brick, brick],
        in_specs=[vmem] * 2,
        out_specs=[pl.BlockSpec(memory_space=pl.ANY), vmem],
        scratch_shapes=[pltpu.VMEM((rows, wide, z), F32)] * 8 + [pltpu.SemaphoreType.DMA],
        compiler_params=pltpu.CompilerParams(vmem_limit_bytes=VMEM_LIMIT),
    )(cond_ext, pot_ext)


def body(image, phases, phase_table, start_potential):
    cond_ext, pot_ext = tensor(image, phases, phase_table, start_potential)
    conductivity, potential = sweeps(cond_ext, pot_ext)
    return conductivity, potential


def solution(mesh):
    placed = (P("gx", "gy", None), P("gx", "gy", None), P(), P("gx", "gy", None))
    return jax.shard_map(
        body,
        mesh=mesh,
        in_specs=placed,
        out_specs=(P("gx", "gy", None), P("gx", "gy", None)),
        check_vma=False,
    )
```

```python
import functools
import math

import jax
import jax.numpy as jnp
import ml_dtypes
import numpy as np
from jax import lax
from jax.experimental import pallas as pl
from jax.experimental.pallas import tpu as pltpu
from jax.sharding import PartitionSpec as P

SWEEPS = 3
PHASES = 3
DERIV = 3
SMOOTH = 12
IMG_X = DERIV + SMOOTH
IMG_Y = 16
POT_X = SWEEPS
POT_Y = 8
MESH = pl.DeviceIdType.MESH
PIECES = 4
VMEM_LIMIT = 32 * 1024 * 1024
F32 = jnp.float32
BF16 = jnp.bfloat16


def gauss_taps(sigma, reach, order):
    values = [math.exp(-t * t / (2.0 * sigma * sigma)) for t in range(-reach, reach + 1)]
    total = sum(values)
    values = [value / total for value in values]
    if order == 1:
        values = [(i - reach) * values[i] / (sigma * sigma) for i in range(2 * reach + 1)]
    return values


NEAR = gauss_taps(1.0, DERIV, 0)
SLOPE = gauss_taps(1.0, DERIV, 1)
WIDE = gauss_taps(4.0, SMOOTH, 0)


def halves(matrix):
    high = matrix.astype(ml_dtypes.bfloat16)
    low = (matrix - high.astype(np.float32)).astype(ml_dtypes.bfloat16)
    return high, low


def band(out_len, in_len, margin, taps, first=0, last=None):
    reach = (len(taps) - 1) // 2
    matrix = np.zeros((out_len, in_len), np.float32)
    for i in range(first, out_len if last is None else last):
        for t in range(-reach, reach + 1):
            k = i + margin + t
            if 0 <= k < in_len:
                matrix[i, k] = taps[t + reach]
    return matrix


def left_weights(matrix):
    high, low = halves(matrix)
    return np.concatenate([high, high, low], axis=1)


def pair_weights(matrix):
    high, low = halves(matrix)
    none = np.zeros_like(high)
    return np.block([
        [high, high, none, none], [low, none, none, none],
        [none, none, high, high], [none, none, low, none]])


def right_weights(*matrices):
    parts = []
    for matrix in matrices:
        parts += list(halves(np.ascontiguousarray(matrix.T)))
    return np.concatenate(parts, axis=1)


def neighbours():
    gx, gy = lax.axis_index("gx"), lax.axis_index("gy")
    nx, ny = lax.axis_size("gx"), lax.axis_size("gy")
    has_x = (gx > 0, gx < nx - 1)
    has_y = (gy > 0, gy < ny - 1)
    at_x = ((gx - 1, gy), (gx + 1, gy))
    at_y = ((gx, gy - 1), (gx, gy + 1))
    return has_x, has_y, at_x, at_y


def greet():
    has_x, has_y, at_x, at_y = neighbours()
    barrier = pltpu.get_barrier_semaphore()
    known = list(zip(has_x + has_y, at_x + at_y))
    for d in range(2):
        for e in range(2):
            known.append((jnp.logical_and(has_x[d], has_y[e]), (at_x[d][0], at_y[e][1])))
    for has, at in known:
        @pl.when(has)
        def _(at=at):
            pl.semaphore_signal(barrier, inc=1, device_id=at, device_id_type=MESH)
    pl.semaphore_wait(barrier, sum(has.astype(jnp.int32) for has, _ in known))


class Exchange:
    def __init__(self, own, ext, hx, hy, cuts, bands, send, recv, middle=False):
        self.ext, self.hx, self.hy, self.cuts, self.bands = ext, hx, hy, cuts, bands
        self.send, self.recv = send, recv
        self.nx, self.ny = ext.shape[0] - 2 * hx, ext.shape[1] - 2 * hy
        self.own = own
        self.has_x, self.has_y, self.at_x, self.at_y = neighbours()
        gy, half = lax.axis_index("gy"), lax.axis_size("gy") // 2
        if middle:
            self.mid = (gy == half, gy == half - 1)
            self.passes = tuple(
                jnp.logical_and(has, jnp.logical_not(mid))
                for has, mid in zip(self.has_y, self.mid))
        else:
            self.mid, self.passes = None, self.has_y

    @staticmethod
    def count(cuts, bands):
        return 2 * len(bands) + 10 * len(cuts)

    def remote(self, src, dst, index, at):
        return pltpu.make_async_remote_copy(
            src_ref=src, dst_ref=dst, send_sem=self.send.at[index],
            recv_sem=self.recv.at[index], device_id=at, device_id_type=MESH)

    def brick(self, row, rows, col, cols):
        if self.own is None:
            return self.ext.at[pl.ds(self.hx + row, rows), pl.ds(self.hy + col, cols)]
        return self.own.at[pl.ds(row, rows), pl.ds(col, cols)]

    def halo_rows(self, d, c):
        size = self.cuts[0][1]
        if d == 0:
            return self.nx + self.hx + c * size, size
        return self.hx - (c + 1) * size, size

    def copy_x(self, d, c, half=None):
        row, size = self.halo_rows(d, c)
        start = c * size if d == 0 else self.nx - (c + 1) * size
        n = len(self.cuts)
        if half is None:
            col, cols, index = 0, self.ny, d * n + c
        else:
            col, cols = half * (self.ny // 2), self.ny // 2
            index = (d if half == 0 else 8 + d) * n + half * 2 * len(self.bands) + c
        return self.remote(
            self.brick(start, size, col, cols),
            self.ext.at[pl.ds(row, size), pl.ds(self.hy + col, cols)],
            index, self.at_x[d])

    def copy_y(self, d, k):
        a, b = self.bands[k]
        src = 0 if d == 0 else self.ny - self.hy
        dst = self.hy + self.ny if d == 0 else 0
        return self.remote(
            self.brick(a, b - a, src, self.hy),
            self.ext.at[pl.ds(self.hx + a, b - a), pl.ds(dst, self.hy)],
            6 * len(self.cuts) + d * len(self.bands) + k, self.at_y[d])

    def copy_corner(self, side, d, c):
        row, size = self.halo_rows(side, c)
        src = self.hy if d == 0 else self.ny
        dst = self.hy + self.ny if d == 0 else 0
        n = len(self.cuts)
        return self.remote(
            self.ext.at[pl.ds(row, size), pl.ds(src, self.hy)],
            self.ext.at[pl.ds(row, size), pl.ds(dst, self.hy)],
            2 * n + (side * 2 + d) * n + c, self.at_y[d])

    def copy_diagonal(self, d, e):
        row, size = self.halo_rows(d, 0)
        return self.remote(
            self.brick(0 if d == 0 else self.nx - size, size,
                       0 if e == 0 else self.ny - self.hy, self.hy),
            self.ext.at[pl.ds(row, size),
                        pl.ds(self.hy + self.ny if e == 0 else 0, self.hy)],
            2 * len(self.cuts) + 2 * d + e, (self.at_x[d][0], self.at_y[e][1]))

    def each_diagonal(self, has_x, has_y, action):
        for d in range(2):
            for e in range(2):
                pl.when(jnp.logical_and(has_x[d], has_y[e]))(
                    lambda d=d, e=e: action(self.copy_diagonal(d, e)))

    def start_diagonal(self):
        self.each_diagonal(self.has_x, self.has_y, lambda copy: copy.start())

    def wait_all(self):
        for d in range(2):
            pl.when(self.has_x[1 - d])(lambda d=d: self.copy_x(d, 0).wait_recv())
        for k in range(len(self.bands)):
            self.wait_y(k)
        self.each_diagonal(
            self.has_x[::-1], self.has_y[::-1], lambda copy: copy.wait_recv())

    def copy_mid(self, side, d, c):
        row, size = self.halo_rows(d, c)
        start = c * size if d == 0 else self.nx - (c + 1) * size
        at = self.hy + self.ny if side == 1 else 0
        return self.remote(
            self.ext.at[pl.ds(self.hx + start, size), pl.ds(at, self.hy)],
            self.ext.at[pl.ds(row, size), pl.ds(at, self.hy)],
            6 * len(self.cuts) + 2 * len(self.bands) + d * len(self.cuts) + c, self.at_x[d])

    def each_mid(self, has, action):
        for side in range(2):
            for d in range(2):
                pl.when(jnp.logical_and(self.mid[side], has[d]))(
                    lambda side=side, d=d: action(side, d))

    def start_mid(self, c):
        self.each_mid(self.has_x, lambda side, d: self.copy_mid(side, d, c).start())

    def wait_mid(self, c):
        self.each_mid(
            self.has_x[::-1], lambda side, d: self.copy_mid(side, d, c).wait_recv())

    def start_x(self, c, half=None):
        for d in range(2):
            pl.when(self.has_x[d])(lambda d=d: self.copy_x(d, c, half).start())

    def sent_x(self, c, half=None):
        for d in range(2):
            pl.when(self.has_x[d])(lambda d=d: self.copy_x(d, c, half).wait_send())

    def start_y(self, k):
        for d in range(2):
            pl.when(self.has_y[d])(lambda d=d: self.copy_y(d, k).start())

    def clear(self):
        rows, cols, z = self.ext.shape
        for d in range(2):
            @pl.when(jnp.logical_not(self.has_x[d]))
            def _(d=d):
                at = 0 if d == 0 else self.hx + self.nx
                self.ext[pl.ds(at, self.hx)] = jnp.zeros((self.hx, cols, z), F32)

            @pl.when(jnp.logical_not(self.has_y[d]))
            def _(d=d):
                at = 0 if d == 0 else self.hy + self.ny
                self.ext[:, pl.ds(at, self.hy)] = jnp.zeros((rows, self.hy, z), F32)

    def forward(self, c):
        for d in range(2):
            for side in range(2):
                @pl.when(self.has_x[1 - side])
                def _(side=side, d=d):
                    self.copy_x(side, c, d).wait_recv()
                    pl.when(self.passes[d])(lambda: self.copy_corner(side, d, c).start())

    def wait_y(self, k):
        for d in range(2):
            pl.when(self.has_y[1 - d])(lambda d=d: self.copy_y(d, k).wait_recv())

    def wait_corner(self, c):
        for side in range(2):
            for d in range(2):
                pl.when(jnp.logical_and(self.has_x[1 - side], self.passes[1 - d]))(
                    lambda d=d, side=side: self.copy_corner(side, d, c).wait_recv())
        if self.mid is not None:
            self.wait_mid(c)

    def wait_sends(self):
        for d in range(2):
            for k in range(len(self.bands)):
                pl.when(self.has_y[d])(lambda d=d, k=k: self.copy_y(d, k).wait_send())
        if self.mid is None:
            self.sent_x(0)
            self.each_diagonal(self.has_x, self.has_y, lambda copy: copy.wait_send())
            return
        for half in range(2):
            self.sent_x(len(self.cuts) - 1, half)
        for c in range(len(self.cuts)):
            for side in range(2):
                for d in range(2):
                    pl.when(jnp.logical_and(self.has_x[1 - side], self.passes[d]))(
                        lambda d=d, c=c, side=side: self.copy_corner(side, d, c).wait_send())
            self.each_mid(
                self.has_x, lambda side, d, c=c: self.copy_mid(side, d, c).wait_send())


def split(value):
    high = value.astype(BF16)
    return high, (value - high.astype(F32)).astype(BF16)


def dot(a, b):
    return jnp.dot(a, b, preferred_element_type=F32)


def left(weights, value):
    high, low = split(value)
    return dot(weights, jnp.concatenate([high, low, high], axis=0))


def right(value, high_w, low_w):
    high, low = split(value)
    return dot(high, high_w) + dot(low, high_w) + dot(high, low_w)


STEP = 5
IMG_CUTS = tuple((a, a + STEP) for a in range(0, IMG_X, STEP))
POT_CUTS = ((0, POT_X),)


def brick_bands(bx):
    return ((0, POT_X), (bx - POT_X, bx), (POT_X, bx - POT_X))


def tensor_kernel(image, phases_in, table_in, start, wg_in, ws_in, zg_in, zs_in, cond, pot,
                  ext, za, zb, grads, masked, along, smooth, phases, table, wg, ws, zg, zs, *sems):
    gx, gy = lax.axis_index("gx"), lax.axis_index("gy")
    bx, by, z = phases.shape
    size_x, size_y = bx * lax.axis_size("gx"), by * lax.axis_size("gy")
    wide_y = ext.shape[1]
    rows_x = bx + 2 * SMOOTH
    bands = brick_bands(bx)

    img = Exchange(image, ext, IMG_X, IMG_Y, IMG_CUTS, ((0, bx),), *sems[0:2], middle=True)
    pots = Exchange(start, pot, POT_X, POT_Y, POT_CUTS, ((0, bx),), *sems[2:4])
    conds = Exchange(None, cond, POT_X, POT_Y, POT_CUTS, bands, *sems[4:6])
    own_image = pltpu.make_async_copy(
        image, ext.at[pl.ds(IMG_X, bx), pl.ds(IMG_Y, by)], sems[6])
    own_start = pltpu.make_async_copy(
        start, pot.at[pl.ds(POT_X, bx), pl.ds(POT_Y, by)], sems[7])

    loads = [
        pltpu.make_async_copy(src, dst, sems[8 + k])
        for k, (src, dst) in enumerate((
            (wg_in, wg), (zg_in, zg), (ws_in, ws), (phases_in, phases), (zs_in, zs),
            (table_in, table)))
    ]
    own_image.start()
    for load in loads:
        load.start()
    greet()
    img.start_x(0, 0)
    img.start_y(0)
    img.start_x(0, 1)
    own_start.start()
    for part in (img, pots, conds):
        part.clear()

    for load in loads[:3]:
        load.wait()
    row_y = gy * by - IMG_Y + lax.broadcasted_iota(jnp.int32, (wide_y, wg.shape[1]), 0)
    inside = jnp.logical_and(row_y >= 0, row_y < size_y)
    for k in range(2):
        part = wg[k * wide_y:(k + 1) * wide_y].astype(F32)
        masked[k * wide_y:(k + 1) * wide_y] = jnp.where(inside, part, 0.0).astype(BF16)
    own_image.wait()

    def along_z(row, rows, col, cols):
        size = rows * cols
        high, low = split(ext[pl.ds(row, rows), pl.ds(col, cols)].reshape(size, z))
        for k, to in enumerate((za, zb)):
            hw, lw = zg[:, 2 * k * z:(2 * k + 1) * z], zg[:, (2 * k + 1) * z:(2 * k + 2) * z]
            out = dot(high, hw) + dot(low, hw) + dot(high, lw)
            to[pl.ds(row, rows), pl.ds(col, cols)] = out.reshape(rows, cols, z)

    def loop(count, action):
        lax.fori_loop(0, count, lambda k, carry: (action(k), carry)[1], 0)

    def gradients(rows, slot):
        for n, r in enumerate(rows):
            at = gx * bx + r - SMOOTH
            ok = jnp.logical_and(at >= 0, at < size_x).astype(F32)
            a = [za[r + t] for t in range(2 * DERIV + 1)]
            b = [zb[r + t] for t in range(2 * DERIV + 1)]
            a_n, b_n = a[DERIV] * (NEAR[DERIV] * ok), b[DERIV] * (NEAR[DERIV] * ok)
            a_s = None
            for t in range(1, DERIV + 1):
                near, slope = NEAR[DERIV + t] * ok, SLOPE[DERIV + t] * ok
                a_n = a_n + (a[DERIV + t] + a[DERIV - t]) * near
                b_n = b_n + (b[DERIV + t] + b[DERIV - t]) * near
                term = (a[DERIV + t] - a[DERIV - t]) * slope
                a_s = term if a_s is None else a_s + term
            grads[slot + 3 * n] = left(masked[:wide_y], a_s)
            grads[slot + 3 * n + 1] = left(masked[wide_y:], a_n)
            grads[slot + 3 * n + 2] = left(masked[:wide_y], b_n)

    def products(rows, slot):
        for n, r in enumerate(rows):
            g = [grads[slot + 3 * n + k] for k in range(3)]
            pairs = ((0, 0), (1, 1), (2, 2), (0, 1), (0, 2), (1, 2))
            for f in range(0, 6, 2):
                parts = []
                for p, q in pairs[f:f + 2]:
                    parts += split(g[p] * g[q])
                out = dot(ws[...], jnp.concatenate(parts, axis=0))
                along[f, r] = out[:by] + out[by:2 * by]
                along[f + 1, r] = out[2 * by:3 * by] + out[3 * by:]

    centre, chunks = rows_x // 2, len(IMG_CUTS)

    def pair_of(k):
        part, j = k // STEP, k % STEP
        return centre - (part + 1) * STEP + j, centre + part * STEP + j

    def derive(part):
        for j in range(STEP + 1):
            if j < STEP:
                gradients(pair_of(part * STEP + j), 6 * j)
            if j > 0:
                products(pair_of(part * STEP + j - 1), 6 * (j - 1))

    tiles_y, tiles_z = by // 8, z // 128

    def smooth_x(known, ready, tiles):
        new = [r in known and r not in ready for r in range(rows_x)]

        def tile(n):
            f = n // (tiles_y * tiles_z)
            ys = pl.ds(pl.multiple_of((n // tiles_z) % tiles_y * 8, 8), 8)
            zz = pl.ds(pl.multiple_of(n % tiles_z * 128, 128), 128)
            v = [along[f, r, ys, zz] if new[r] else None for r in range(rows_x)]
            for i in range(bx):
                c = i + SMOOTH
                terms = [v[c] * WIDE[SMOOTH]] if new[c] else []
                for t in range(1, SMOOTH + 1):
                    pair = [v[r] for r in (c + t, c - t) if new[r]]
                    if pair:
                        terms.append((pair[0] + pair[1] if len(pair) > 1 else pair[0])
                                     * WIDE[SMOOTH + t])
                if terms:
                    total = smooth[f, i, ys, zz] if ready else terms.pop(0)
                    for term in terms:
                        total = total + term
                    smooth[f, i, ys, zz] = total

        def step(n):
            for k in range(tiles):
                tile(n * tiles + k)
        loop(6 * tiles_y * tiles_z // tiles, step)

    along_z(IMG_X, bx, IMG_Y, by)
    img.sent_x(0, 0)
    img.start_x(1, 0)
    img.sent_x(0, 1)
    img.start_x(1, 1)
    img.wait_y(0)
    img.start_mid(0)
    img.forward(0)
    img.sent_x(1, 0)
    img.start_x(2, 0)
    along_z(IMG_X, bx, 0, IMG_Y)
    along_z(IMG_X, bx, IMG_Y + by, IMG_Y)
    img.start_mid(1)
    img.sent_x(1, 1)
    img.start_x(2, 1)
    img.start_mid(2)
    core = range(chunks * STEP, rows_x - chunks * STEP)
    inner = range(STEP, rows_x - STEP)

    def segment(part):
        @pl.when(part == chunks)
        def _():
            pots.start_y(0)
            pots.start_diagonal()
            smooth_x(inner, core, 4)

        @pl.when(part > 0)
        def _():
            c = part - 1
            pl.when(part < chunks)(lambda: img.forward(c + 1))
            pl.when(part == 1)(lambda: smooth_x(core, (), 4))

            @pl.when(part == chunks - 1)
            def _():
                pots.start_x(0)
            img.wait_corner(c)
            along_z(bx + IMG_X + c * STEP, STEP, 0, wide_y)
            along_z(IMG_X - (c + 1) * STEP, STEP, 0, wide_y)
        derive(part)

    loop(chunks + 1, segment)
    smooth_x(range(rows_x), inner, 4)
    for load in loads[3:]:
        load.wait()

    def along_z_last(parts, slot):
        every = right(
            jnp.concatenate([smooth[f, i, a:b] for i, a, b in parts for f in range(6)], axis=0),
            zs[:, :z], zs[:, z:])
        at = 0
        for n, (i, a, b) in enumerate(parts):
            for f in range(6):
                grads[slot + f, n * 16:n * 16 + b - a] = every[at:at + b - a]
                at += b - a

    def weigh(parts, slot):
        for n, (i, a, b) in enumerate(parts):
            jxx, jyy, jzz, jxy, jxz, jyz = (
                grads[slot + f, n * 16:n * 16 + b - a] for f in range(6))
            trace = jxx + jyy + jzz
            shift = 0.1 * trace + 1e-06
            p, q, c = jxx + shift, jyy + shift, jzz + shift
            cof = p * q - jxy * jxy
            det = (
                p * (q * c - jyz * jyz)
                - jxy * (jxy * c - jyz * jxz)
                + jxz * (jxy * jyz - q * jxz)
            )
            weight = trace * cof / det
            label = phases[i, a:b]
            base = jnp.where(
                label == 0, table[0, 0], jnp.where(label == 1, table[0, 1], table[0, 2]))
            aniso = jnp.where(
                label == 0, table[1, 0], jnp.where(label == 1, table[1, 1], table[1, 2]))
            cond[POT_X + i, POT_Y + a:POT_Y + b] = base + 0.1 * aniso * weight

    outer = list(range(POT_X)) + list(range(bx - POT_X, bx))
    rest = range(POT_X, bx - POT_X)
    half = by // 2
    units = [[(i, 0, half), (i, half, by)] for i in outer]
    units = [units[k] + units[k + 1] for k in range(0, len(units), 2)]
    first = len(units)
    edges = [[(i, 0, POT_Y), (i, by - POT_Y, by)] for i in rest]
    units += [edges[k] + edges[k + 1] for k in range(0, len(edges), 2)]
    second = len(units)
    middle = [[(i, POT_Y, by - POT_Y)] for i in rest]
    units += [middle[k] + middle[k + 1] for k in range(0, len(middle), 2)]
    for k in range(len(units) + 1):
        if k < len(units):
            along_z_last(units[k], 6 * (k % STEP))
        if k > 0:
            weigh(units[k - 1], 6 * ((k - 1) % STEP))
        if k == first:
            conds.start_x(0)
            conds.start_diagonal()
            conds.start_y(0)
            conds.start_y(1)
        if k == second:
            conds.start_y(2)


    own_start.wait()
    pots.wait_all()
    conds.wait_all()
    for part in (img, pots, conds):
        part.wait_sends()


def tensor(image, phases, table, start):
    bx, by, z = phases.shape
    wide_y = by + 2 * IMG_Y
    rows_x = bx + 2 * SMOOTH
    lo, hi = IMG_Y - SMOOTH, wide_y - (IMG_Y - SMOOTH)
    wg = np.concatenate([
        left_weights(band(wide_y, wide_y, 0, NEAR, lo, hi)),
        left_weights(band(wide_y, wide_y, 0, SLOPE, lo, hi)),
    ], axis=0)
    ws = pair_weights(band(by, wide_y, IMG_Y, WIDE))
    zg = right_weights(band(z, z, 0, NEAR), band(z, z, 0, SLOPE))
    zs = right_weights(band(z, z, 0, WIDE))
    vmem = pl.BlockSpec(memory_space=pltpu.VMEM)
    anywhere = pl.BlockSpec(memory_space=pltpu.HBM)
    outer = jax.ShapeDtypeStruct((bx + 2 * POT_X, by + 2 * POT_Y, z), F32)
    sems = []
    for count in (
        Exchange.count(IMG_CUTS, ((0, bx),)),
        Exchange.count(POT_CUTS, ((0, bx),)),
        Exchange.count(POT_CUTS, brick_bands(bx)),
    ):
        sems += [pltpu.SemaphoreType.DMA((count,))] * 2
    return pl.pallas_call(
        tensor_kernel,
        out_shape=[outer, outer],
        in_specs=[anywhere] * 8,
        out_specs=[vmem, vmem],
        scratch_shapes=[
            pltpu.VMEM((bx + 2 * IMG_X, wide_y, z), F32),
            pltpu.VMEM((bx + 2 * IMG_X, wide_y, z), F32),
            pltpu.VMEM((bx + 2 * IMG_X, wide_y, z), F32),
            pltpu.VMEM((6 * STEP, wide_y, z), F32),
            pltpu.VMEM(wg.shape, BF16),
            pltpu.VMEM((6, rows_x, by, z), F32),
            pltpu.VMEM((6, bx, by, z), F32),
            pltpu.VMEM(phases.shape, jnp.int32),
            pltpu.SMEM(table.shape, F32),
        ] + [pltpu.VMEM(w.shape, BF16) for w in (wg, ws, zg, zs)]
        + sems + [pltpu.SemaphoreType.DMA] * 8,
        compiler_params=pltpu.CompilerParams(
            collective_id=0, has_side_effects=True, vmem_limit_bytes=VMEM_LIMIT),
    )(*(pltpu.with_memory_space_constraint(jnp.asarray(x), pltpu.HBM)
        for x in (image, phases, table, start, wg, ws, zg, zs)))


def harmonic(p, q):
    total = p + q
    return 2.0 * p * q / jnp.where(total > 0, total, 1.0)


def step_of(count):
    return max(n for n in (1, 2, 3, 4) if count % n == 0)


def sweep_kernel(cond, start, centre, out, kx, y0, y1, z0, z1, inv, one, two, three,
                 *sems):
    rows, wide, z = cond.shape
    copy = pltpu.make_async_copy(
        cond.at[pl.ds(POT_X, rows - 2 * POT_X), pl.ds(POT_Y, wide - 2 * POT_Y)], centre, sems[0])
    copy.start()
    lane = lax.broadcasted_iota(jnp.int32, (1, wide, z), 2)
    at_low, at_high = lane == 0, lane == z - 1

    def roll_y(v, s):
        return pltpu.roll(v, s % wide, 1)

    def roll_z(v, s):
        return pltpu.roll(v, s % z, 2)

    kx[0] = harmonic(cond[0], cond[1])
    size = 2

    def coefficients(step, carry):
        j = 1 + step * size
        c = cond[pl.ds(j, size)]
        x_up = harmonic(c, cond[pl.ds(j + 1, size)])
        y_up = harmonic(c, roll_y(c, -1))
        z_up = harmonic(c, roll_z(c, -1))
        x_down = jnp.concatenate([kx[j - 1][None], x_up[:size - 1]], axis=0)
        y_down = roll_y(y_up, 1)
        low = jnp.where(at_low, c, roll_z(z_up, 1))
        high = jnp.where(at_high, c, z_up)
        total = x_down + x_up + y_down + y_up + low + high
        kx[pl.ds(j, size)] = x_up
        y0[pl.ds(j, size)] = y_down
        y1[pl.ds(j, size)] = y_up
        z0[pl.ds(j, size)] = low
        z1[pl.ds(j, size)] = jnp.where(at_high, 0.0, z_up)
        inv[pl.ds(j, size)] = 1.0 / jnp.where(total > 0, total, 1.0)
        return carry

    lax.fori_loop(0, (rows - 2) // size, coefficients, 0)

    def relaxed(src, j, size, first, last):
        at, cols = pl.ds(j, size), pl.ds(first, last - first)
        p = src[at]
        own = p[:, first:last]
        if first > 0:
            below, above = p[:, first - 1:last - 1], p[:, first + 1:last + 1]
        else:
            below, above = roll_y(p, 1), roll_y(p, -1)
        numer = kx[pl.ds(j - 1, size), cols] * src[pl.ds(j - 1, size), cols]
        numer = numer + kx[at, cols] * src[pl.ds(j + 1, size), cols]
        numer = numer + y0[at, cols] * below + y1[at, cols] * above
        numer = numer + z0[at, cols] * jnp.where(at_low[:, first:last], 1.0, roll_z(own, 1))
        numer = numer + z1[at, cols] * roll_z(own, -1)
        return numer * inv[at, cols]

    def sweep(src, dst, first, last):
        size = step_of(last - first)

        def step(k, carry):
            j = first + k * size
            dst[pl.ds(j, size)] = relaxed(src, j, size, 0, wide)
            return carry
        lax.fori_loop(0, (last - first) // size, step, 0)

    sweep(start, one, 1, rows - 1)
    sweep(one, two, 2, rows - 2)
    brick = rows - 2 * POT_X
    size = brick // PIECES
    sends = []
    for k in range(PIECES):
        part = pl.ds(k * size, size)
        three[part] = relaxed(two, POT_X + k * size, size, POT_Y, wide - POT_Y)
        sends.append(pltpu.make_async_copy(three.at[part], out.at[part], sems[1 + k]))
        sends[-1].start()
    copy.wait()
    for send in sends:
        send.wait()


def sweeps(cond_ext, pot_ext):
    rows, wide, z = cond_ext.shape
    vmem = pl.BlockSpec(memory_space=pltpu.VMEM)
    brick = jax.ShapeDtypeStruct((rows - 2 * POT_X, wide - 2 * POT_Y, z), F32)
    return pl.pallas_call(
        sweep_kernel,
        out_shape=[brick, brick],
        in_specs=[vmem] * 2,
        out_specs=[pl.BlockSpec(memory_space=pl.ANY)] * 2,
        scratch_shapes=[pltpu.VMEM((rows, wide, z), F32)] * 8 + [
            pltpu.VMEM(brick.shape, F32)] + [pltpu.SemaphoreType.DMA] * (1 + PIECES),
        compiler_params=pltpu.CompilerParams(vmem_limit_bytes=VMEM_LIMIT),
    )(cond_ext, pot_ext)


def body(image, phases, phase_table, start_potential):
    cond_ext, pot_ext = tensor(image, phases, phase_table, start_potential)
    conductivity, potential = sweeps(cond_ext, pot_ext)
    return conductivity, potential


def solution(mesh):
    placed = (P("gx", "gy", None), P("gx", "gy", None), P(), P("gx", "gy", None))
    return jax.shard_map(
        body,
        mesh=mesh,
        in_specs=placed,
        out_specs=(P("gx", "gy", None), P("gx", "gy", None)),
        check_vma=False,
    )
```

```python
import functools
import math

import jax
import jax.numpy as jnp
import ml_dtypes
import numpy as np
from jax import lax
from jax.experimental import pallas as pl
from jax.experimental.pallas import tpu as pltpu
from jax.sharding import PartitionSpec as P

SWEEPS = 3
PHASES = 3
DERIV = 3
SMOOTH = 12
IMG_X = DERIV + SMOOTH
IMG_Y = 16
POT_X = SWEEPS
POT_Y = 8
MESH = pl.DeviceIdType.MESH
PIECES = 4
VMEM_LIMIT = 32 * 1024 * 1024
F32 = jnp.float32
BF16 = jnp.bfloat16


def gauss_taps(sigma, reach, order):
    values = [math.exp(-t * t / (2.0 * sigma * sigma)) for t in range(-reach, reach + 1)]
    total = sum(values)
    values = [value / total for value in values]
    if order == 1:
        values = [(i - reach) * values[i] / (sigma * sigma) for i in range(2 * reach + 1)]
    return values


NEAR = gauss_taps(1.0, DERIV, 0)
SLOPE = gauss_taps(1.0, DERIV, 1)
WIDE = gauss_taps(4.0, SMOOTH, 0)


def halves(matrix):
    high = matrix.astype(ml_dtypes.bfloat16)
    low = (matrix - high.astype(np.float32)).astype(ml_dtypes.bfloat16)
    return high, low


def band(out_len, in_len, margin, taps, first=0, last=None):
    reach = (len(taps) - 1) // 2
    matrix = np.zeros((out_len, in_len), np.float32)
    for i in range(first, out_len if last is None else last):
        for t in range(-reach, reach + 1):
            k = i + margin + t
            if 0 <= k < in_len:
                matrix[i, k] = taps[t + reach]
    return matrix


def left_weights(matrix):
    high, low = halves(matrix)
    return np.concatenate([high, high, low], axis=1)


def pair_weights(matrix):
    high, low = halves(matrix)
    none = np.zeros_like(high)
    return np.block([
        [high, high, none, none], [low, none, none, none],
        [none, none, high, high], [none, none, low, none]])


def right_weights(*matrices):
    parts = []
    for matrix in matrices:
        parts += list(halves(np.ascontiguousarray(matrix.T)))
    return np.concatenate(parts, axis=1)


def neighbours():
    gx, gy = lax.axis_index("gx"), lax.axis_index("gy")
    nx, ny = lax.axis_size("gx"), lax.axis_size("gy")
    has_x = (gx > 0, gx < nx - 1)
    has_y = (gy > 0, gy < ny - 1)
    at_x = ((gx - 1, gy), (gx + 1, gy))
    at_y = ((gx, gy - 1), (gx, gy + 1))
    return has_x, has_y, at_x, at_y


def greet():
    has_x, has_y, at_x, at_y = neighbours()
    barrier = pltpu.get_barrier_semaphore()
    known = list(zip(has_x + has_y, at_x + at_y))
    for d in range(2):
        for e in range(2):
            known.append((jnp.logical_and(has_x[d], has_y[e]), (at_x[d][0], at_y[e][1])))
    for has, at in known:
        @pl.when(has)
        def _(at=at):
            pl.semaphore_signal(barrier, inc=1, device_id=at, device_id_type=MESH)
    pl.semaphore_wait(barrier, sum(has.astype(jnp.int32) for has, _ in known))


class Exchange:
    def __init__(self, own, ext, hx, hy, cuts, bands, send, recv, middle=False):
        self.ext, self.hx, self.hy, self.cuts, self.bands = ext, hx, hy, cuts, bands
        self.send, self.recv = send, recv
        self.nx, self.ny = ext.shape[0] - 2 * hx, ext.shape[1] - 2 * hy
        self.own = own
        self.has_x, self.has_y, self.at_x, self.at_y = neighbours()
        gy, half = lax.axis_index("gy"), lax.axis_size("gy") // 2
        if middle:
            self.mid = (gy == half, gy == half - 1)
            self.passes = tuple(
                jnp.logical_and(has, jnp.logical_not(mid))
                for has, mid in zip(self.has_y, self.mid))
        else:
            self.mid, self.passes = None, self.has_y

    @staticmethod
    def count(cuts, bands):
        return 2 * len(bands) + 10 * len(cuts)

    def remote(self, src, dst, index, at):
        return pltpu.make_async_remote_copy(
            src_ref=src, dst_ref=dst, send_sem=self.send.at[index],
            recv_sem=self.recv.at[index], device_id=at, device_id_type=MESH)

    def brick(self, row, rows, col, cols):
        if self.own is None:
            return self.ext.at[pl.ds(self.hx + row, rows), pl.ds(self.hy + col, cols)]
        return self.own.at[pl.ds(row, rows), pl.ds(col, cols)]

    def halo_rows(self, d, c):
        size = self.cuts[0][1]
        if d == 0:
            return self.nx + self.hx + c * size, size
        return self.hx - (c + 1) * size, size

    def copy_x(self, d, c, half=None):
        row, size = self.halo_rows(d, c)
        start = c * size if d == 0 else self.nx - (c + 1) * size
        n = len(self.cuts)
        if half is None:
            col, cols, index = 0, self.ny, d * n + c
        else:
            col, cols = half * (self.ny // 2), self.ny // 2
            index = (d if half == 0 else 8 + d) * n + half * 2 * len(self.bands) + c
        return self.remote(
            self.brick(start, size, col, cols),
            self.ext.at[pl.ds(row, size), pl.ds(self.hy + col, cols)],
            index, self.at_x[d])

    def copy_y(self, d, k):
        a, b = self.bands[k]
        src = 0 if d == 0 else self.ny - self.hy
        dst = self.hy + self.ny if d == 0 else 0
        return self.remote(
            self.brick(a, b - a, src, self.hy),
            self.ext.at[pl.ds(self.hx + a, b - a), pl.ds(dst, self.hy)],
            6 * len(self.cuts) + d * len(self.bands) + k, self.at_y[d])

    def copy_corner(self, side, d, c):
        row, size = self.halo_rows(side, c)
        src = self.hy if d == 0 else self.ny
        dst = self.hy + self.ny if d == 0 else 0
        n = len(self.cuts)
        return self.remote(
            self.ext.at[pl.ds(row, size), pl.ds(src, self.hy)],
            self.ext.at[pl.ds(row, size), pl.ds(dst, self.hy)],
            2 * n + (side * 2 + d) * n + c, self.at_y[d])

    def copy_diagonal(self, d, e):
        row, size = self.halo_rows(d, 0)
        return self.remote(
            self.brick(0 if d == 0 else self.nx - size, size,
                       0 if e == 0 else self.ny - self.hy, self.hy),
            self.ext.at[pl.ds(row, size),
                        pl.ds(self.hy + self.ny if e == 0 else 0, self.hy)],
            2 * len(self.cuts) + 2 * d + e, (self.at_x[d][0], self.at_y[e][1]))

    def each_diagonal(self, has_x, has_y, action):
        for d in range(2):
            for e in range(2):
                pl.when(jnp.logical_and(has_x[d], has_y[e]))(
                    lambda d=d, e=e: action(self.copy_diagonal(d, e)))

    def start_diagonal(self):
        self.each_diagonal(self.has_x, self.has_y, lambda copy: copy.start())

    def wait_all(self):
        for d in range(2):
            pl.when(self.has_x[1 - d])(lambda d=d: self.copy_x(d, 0).wait_recv())
        for k in range(len(self.bands)):
            self.wait_y(k)
        self.each_diagonal(
            self.has_x[::-1], self.has_y[::-1], lambda copy: copy.wait_recv())

    def copy_mid(self, side, d, c):
        row, size = self.halo_rows(d, c)
        start = c * size if d == 0 else self.nx - (c + 1) * size
        at = self.hy + self.ny if side == 1 else 0
        return self.remote(
            self.ext.at[pl.ds(self.hx + start, size), pl.ds(at, self.hy)],
            self.ext.at[pl.ds(row, size), pl.ds(at, self.hy)],
            6 * len(self.cuts) + 2 * len(self.bands) + d * len(self.cuts) + c, self.at_x[d])

    def each_mid(self, has, action):
        for side in range(2):
            for d in range(2):
                pl.when(jnp.logical_and(self.mid[side], has[d]))(
                    lambda side=side, d=d: action(side, d))

    def start_mid(self, c):
        self.each_mid(self.has_x, lambda side, d: self.copy_mid(side, d, c).start())

    def wait_mid(self, c):
        self.each_mid(
            self.has_x[::-1], lambda side, d: self.copy_mid(side, d, c).wait_recv())

    def start_x(self, c, half=None):
        for d in range(2):
            pl.when(self.has_x[d])(lambda d=d: self.copy_x(d, c, half).start())

    def sent_x(self, c, half=None):
        for d in range(2):
            pl.when(self.has_x[d])(lambda d=d: self.copy_x(d, c, half).wait_send())

    def start_y(self, k):
        for d in range(2):
            pl.when(self.has_y[d])(lambda d=d: self.copy_y(d, k).start())

    def clear(self):
        rows, cols, z = self.ext.shape
        for d in range(2):
            @pl.when(jnp.logical_not(self.has_x[d]))
            def _(d=d):
                at = 0 if d == 0 else self.hx + self.nx
                self.ext[pl.ds(at, self.hx)] = jnp.zeros((self.hx, cols, z), F32)

            @pl.when(jnp.logical_not(self.has_y[d]))
            def _(d=d):
                at = 0 if d == 0 else self.hy + self.ny
                self.ext[:, pl.ds(at, self.hy)] = jnp.zeros((rows, self.hy, z), F32)

    def forward(self, c):
        for d in range(2):
            for side in range(2):
                @pl.when(self.has_x[1 - side])
                def _(side=side, d=d):
                    self.copy_x(side, c, d).wait_recv()
                    pl.when(self.passes[d])(lambda: self.copy_corner(side, d, c).start())

    def wait_y(self, k):
        for d in range(2):
            pl.when(self.has_y[1 - d])(lambda d=d: self.copy_y(d, k).wait_recv())

    def wait_corner(self, c):
        for side in range(2):
            for d in range(2):
                pl.when(jnp.logical_and(self.has_x[1 - side], self.passes[1 - d]))(
                    lambda d=d, side=side: self.copy_corner(side, d, c).wait_recv())
        if self.mid is not None:
            self.wait_mid(c)

    def wait_sends(self):
        for d in range(2):
            for k in range(len(self.bands)):
                pl.when(self.has_y[d])(lambda d=d, k=k: self.copy_y(d, k).wait_send())
        if self.mid is None:
            self.sent_x(0)
            self.each_diagonal(self.has_x, self.has_y, lambda copy: copy.wait_send())
            return
        for half in range(2):
            self.sent_x(len(self.cuts) - 1, half)
        for c in range(len(self.cuts)):
            for side in range(2):
                for d in range(2):
                    pl.when(jnp.logical_and(self.has_x[1 - side], self.passes[d]))(
                        lambda d=d, c=c, side=side: self.copy_corner(side, d, c).wait_send())
            self.each_mid(
                self.has_x, lambda side, d, c=c: self.copy_mid(side, d, c).wait_send())


def split(value):
    high = value.astype(BF16)
    return high, (value - high.astype(F32)).astype(BF16)


def dot(a, b):
    return jnp.dot(a, b, preferred_element_type=F32)


def left(weights, value):
    high, low = split(value)
    return dot(weights, jnp.concatenate([high, low, high], axis=0))


def right(value, high_w, low_w):
    high, low = split(value)
    return dot(high, high_w) + dot(low, high_w) + dot(high, low_w)


STEP = 5
IMG_CUTS = tuple((a, a + STEP) for a in range(0, IMG_X, STEP))
POT_CUTS = ((0, POT_X),)


def brick_bands(bx):
    return ((0, POT_X), (bx - POT_X, bx), (POT_X, bx - POT_X))


def tensor_kernel(image, phases_in, table_in, start, wg_in, ws_in, zg_in, zs_in, cond, pot,
                  ext, za, zb, grads, masked, along, smooth, phases, table, wg, ws, zg, zs, *sems):
    gx, gy = lax.axis_index("gx"), lax.axis_index("gy")
    bx, by, z = phases.shape
    size_x, size_y = bx * lax.axis_size("gx"), by * lax.axis_size("gy")
    wide_y = ext.shape[1]
    rows_x = bx + 2 * SMOOTH
    bands = brick_bands(bx)

    img = Exchange(image, ext, IMG_X, IMG_Y, IMG_CUTS, ((0, bx),), *sems[0:2], middle=True)
    pots = Exchange(start, pot, POT_X, POT_Y, POT_CUTS, ((0, bx),), *sems[2:4])
    conds = Exchange(None, cond, POT_X, POT_Y, POT_CUTS, bands, *sems[4:6])
    own_image = pltpu.make_async_copy(
        image, ext.at[pl.ds(IMG_X, bx), pl.ds(IMG_Y, by)], sems[6])
    own_start = pltpu.make_async_copy(
        start, pot.at[pl.ds(POT_X, bx), pl.ds(POT_Y, by)], sems[7])

    loads = [
        pltpu.make_async_copy(src, dst, sems[8 + k])
        for k, (src, dst) in enumerate((
            (wg_in, wg), (zg_in, zg), (ws_in, ws), (phases_in, phases), (zs_in, zs),
            (table_in, table)))
    ]
    own_image.start()
    for load in loads:
        load.start()
    greet()
    img.start_y(0)
    img.start_x(0, 0)
    img.start_x(0, 1)
    own_start.start()
    for part in (img, pots, conds):
        part.clear()

    for load in loads[:3]:
        load.wait()
    row_y = gy * by - IMG_Y + lax.broadcasted_iota(jnp.int32, (wide_y, wg.shape[1]), 0)
    inside = jnp.logical_and(row_y >= 0, row_y < size_y)
    for k in range(2):
        part = wg[k * wide_y:(k + 1) * wide_y].astype(F32)
        masked[k * wide_y:(k + 1) * wide_y] = jnp.where(inside, part, 0.0).astype(BF16)
    own_image.wait()

    def along_z(row, rows, col, cols):
        size = rows * cols
        high, low = split(ext[pl.ds(row, rows), pl.ds(col, cols)].reshape(size, z))
        for k, to in enumerate((za, zb)):
            hw, lw = zg[:, 2 * k * z:(2 * k + 1) * z], zg[:, (2 * k + 1) * z:(2 * k + 2) * z]
            out = dot(high, hw) + dot(low, hw) + dot(high, lw)
            to[pl.ds(row, rows), pl.ds(col, cols)] = out.reshape(rows, cols, z)

    def loop(count, action):
        lax.fori_loop(0, count, lambda k, carry: (action(k), carry)[1], 0)

    def gradients(rows, slot):
        for n, r in enumerate(rows):
            at = gx * bx + r - SMOOTH
            ok = jnp.logical_and(at >= 0, at < size_x).astype(F32)
            a = [za[r + t] for t in range(2 * DERIV + 1)]
            b = [zb[r + t] for t in range(2 * DERIV + 1)]
            a_n, b_n = a[DERIV] * (NEAR[DERIV] * ok), b[DERIV] * (NEAR[DERIV] * ok)
            a_s = None
            for t in range(1, DERIV + 1):
                near, slope = NEAR[DERIV + t] * ok, SLOPE[DERIV + t] * ok
                a_n = a_n + (a[DERIV + t] + a[DERIV - t]) * near
                b_n = b_n + (b[DERIV + t] + b[DERIV - t]) * near
                term = (a[DERIV + t] - a[DERIV - t]) * slope
                a_s = term if a_s is None else a_s + term
            grads[slot + 3 * n] = left(masked[:wide_y], a_s)
            grads[slot + 3 * n + 1] = left(masked[wide_y:], a_n)
            grads[slot + 3 * n + 2] = left(masked[:wide_y], b_n)

    def products(rows, slot):
        for n, r in enumerate(rows):
            g = [grads[slot + 3 * n + k] for k in range(3)]
            pairs = ((0, 0), (1, 1), (2, 2), (0, 1), (0, 2), (1, 2))
            for f in range(0, 6, 2):
                parts = []
                for p, q in pairs[f:f + 2]:
                    parts += split(g[p] * g[q])
                out = dot(ws[...], jnp.concatenate(parts, axis=0))
                along[f, r] = out[:by] + out[by:2 * by]
                along[f + 1, r] = out[2 * by:3 * by] + out[3 * by:]

    centre, chunks = rows_x // 2, len(IMG_CUTS)

    def pair_of(k):
        part, j = k // STEP, k % STEP
        return centre - (part + 1) * STEP + j, centre + part * STEP + j

    def derive(part):
        for j in range(STEP + 1):
            if j < STEP:
                gradients(pair_of(part * STEP + j), 6 * j)
            if j > 0:
                products(pair_of(part * STEP + j - 1), 6 * (j - 1))

    tiles_y, tiles_z = by // 8, z // 128

    def smooth_x(known, ready, tiles):
        new = [r in known and r not in ready for r in range(rows_x)]

        def tile(n):
            f = n // (tiles_y * tiles_z)
            ys = pl.ds(pl.multiple_of((n // tiles_z) % tiles_y * 8, 8), 8)
            zz = pl.ds(pl.multiple_of(n % tiles_z * 128, 128), 128)
            v = [along[f, r, ys, zz] if new[r] else None for r in range(rows_x)]
            for i in range(bx):
                c = i + SMOOTH
                terms = [v[c] * WIDE[SMOOTH]] if new[c] else []
                for t in range(1, SMOOTH + 1):
                    pair = [v[r] for r in (c + t, c - t) if new[r]]
                    if pair:
                        terms.append((pair[0] + pair[1] if len(pair) > 1 else pair[0])
                                     * WIDE[SMOOTH + t])
                if terms:
                    total = smooth[f, i, ys, zz] if ready else terms.pop(0)
                    for term in terms:
                        total = total + term
                    smooth[f, i, ys, zz] = total

        def step(n):
            for k in range(tiles):
                tile(n * tiles + k)
        loop(6 * tiles_y * tiles_z // tiles, step)

    along_z(IMG_X, bx, IMG_Y, by)
    img.sent_x(0, 0)
    img.start_x(1, 0)
    img.sent_x(0, 1)
    img.start_x(1, 1)
    img.wait_y(0)
    img.start_mid(0)
    img.forward(0)
    img.sent_x(1, 0)
    img.start_x(2, 0)
    img.start_mid(1)
    along_z(IMG_X, bx, 0, IMG_Y)
    along_z(IMG_X, bx, IMG_Y + by, IMG_Y)
    img.sent_x(1, 1)
    img.start_x(2, 1)
    img.start_mid(2)
    core = range(chunks * STEP, rows_x - chunks * STEP)
    inner = range(STEP, rows_x - STEP)

    def segment(part):
        @pl.when(part == chunks)
        def _():
            pots.start_x(0)
            pots.start_y(0)
            pots.start_diagonal()
            smooth_x(inner, core, 4)

        @pl.when(part > 0)
        def _():
            c = part - 1
            pl.when(part < chunks)(lambda: img.forward(c + 1))
            pl.when(part == 1)(lambda: smooth_x(core, (), 2))

            img.wait_corner(c)
            along_z(bx + IMG_X + c * STEP, STEP, 0, wide_y)
            along_z(IMG_X - (c + 1) * STEP, STEP, 0, wide_y)
        derive(part)

    loop(chunks + 1, segment)
    smooth_x(range(rows_x), inner, 4)
    for load in loads[3:]:
        load.wait()

    def along_z_last(parts, slot):
        every = right(
            jnp.concatenate([smooth[f, i, a:b] for i, a, b in parts for f in range(6)], axis=0),
            zs[:, :z], zs[:, z:])
        at = 0
        for n, (i, a, b) in enumerate(parts):
            for f in range(6):
                grads[slot + f, n * 16:n * 16 + b - a] = every[at:at + b - a]
                at += b - a

    def weigh(parts, slot):
        for n, (i, a, b) in enumerate(parts):
            jxx, jyy, jzz, jxy, jxz, jyz = (
                grads[slot + f, n * 16:n * 16 + b - a] for f in range(6))
            trace = jxx + jyy + jzz
            shift = 0.1 * trace + 1e-06
            p, q, c = jxx + shift, jyy + shift, jzz + shift
            cof = p * q - jxy * jxy
            det = (
                p * (q * c - jyz * jyz)
                - jxy * (jxy * c - jyz * jxz)
                + jxz * (jxy * jyz - q * jxz)
            )
            weight = trace * cof / det
            label = phases[i, a:b]
            base = jnp.where(
                label == 0, table[0, 0], jnp.where(label == 1, table[0, 1], table[0, 2]))
            aniso = jnp.where(
                label == 0, table[1, 0], jnp.where(label == 1, table[1, 1], table[1, 2]))
            cond[POT_X + i, POT_Y + a:POT_Y + b] = base + 0.1 * aniso * weight

    outer = list(range(POT_X)) + list(range(bx - POT_X, bx))
    rest = range(POT_X, bx - POT_X)
    half = by // 2
    units = [[(i, 0, half), (i, half, by)] for i in outer]
    units = [units[k] + units[k + 1] for k in range(0, len(units), 2)]
    first = len(units)
    edges = [[(i, 0, POT_Y), (i, by - POT_Y, by)] for i in rest]
    units += [edges[k] + edges[k + 1] for k in range(0, len(edges), 2)]
    second = len(units)
    middle = [[(i, POT_Y, by - POT_Y)] for i in rest]
    units += [middle[k] + middle[k + 1] for k in range(0, len(middle), 2)]
    for k in range(len(units) + 1):
        if k < len(units):
            along_z_last(units[k], 6 * (k % STEP))
        if k > 0:
            weigh(units[k - 1], 6 * ((k - 1) % STEP))
        if k == first:
            conds.start_x(0)
            conds.start_diagonal()
            conds.start_y(0)
            conds.start_y(1)
        if k == second:
            conds.start_y(2)


    own_start.wait()
    pots.wait_all()
    conds.wait_all()
    for part in (img, pots, conds):
        part.wait_sends()


def tensor(image, phases, table, start):
    bx, by, z = phases.shape
    wide_y = by + 2 * IMG_Y
    rows_x = bx + 2 * SMOOTH
    lo, hi = IMG_Y - SMOOTH, wide_y - (IMG_Y - SMOOTH)
    wg = np.concatenate([
        left_weights(band(wide_y, wide_y, 0, NEAR, lo, hi)),
        left_weights(band(wide_y, wide_y, 0, SLOPE, lo, hi)),
    ], axis=0)
    ws = pair_weights(band(by, wide_y, IMG_Y, WIDE))
    zg = right_weights(band(z, z, 0, NEAR), band(z, z, 0, SLOPE))
    zs = right_weights(band(z, z, 0, WIDE))
    vmem = pl.BlockSpec(memory_space=pltpu.VMEM)
    anywhere = pl.BlockSpec(memory_space=pltpu.HBM)
    outer = jax.ShapeDtypeStruct((bx + 2 * POT_X, by + 2 * POT_Y, z), F32)
    sems = []
    for count in (
        Exchange.count(IMG_CUTS, ((0, bx),)),
        Exchange.count(POT_CUTS, ((0, bx),)),
        Exchange.count(POT_CUTS, brick_bands(bx)),
    ):
        sems += [pltpu.SemaphoreType.DMA((count,))] * 2
    return pl.pallas_call(
        tensor_kernel,
        out_shape=[outer, outer],
        in_specs=[anywhere] * 8,
        out_specs=[vmem, vmem],
        scratch_shapes=[
            pltpu.VMEM((bx + 2 * IMG_X, wide_y, z), F32),
            pltpu.VMEM((bx + 2 * IMG_X, wide_y, z), F32),
            pltpu.VMEM((bx + 2 * IMG_X, wide_y, z), F32),
            pltpu.VMEM((6 * STEP, wide_y, z), F32),
            pltpu.VMEM(wg.shape, BF16),
            pltpu.VMEM((6, rows_x, by, z), F32),
            pltpu.VMEM((6, bx, by, z), F32),
            pltpu.VMEM(phases.shape, jnp.int32),
            pltpu.SMEM(table.shape, F32),
        ] + [pltpu.VMEM(w.shape, BF16) for w in (wg, ws, zg, zs)]
        + sems + [pltpu.SemaphoreType.DMA] * 8,
        compiler_params=pltpu.CompilerParams(
            collective_id=0, has_side_effects=True, vmem_limit_bytes=VMEM_LIMIT),
    )(*(pltpu.with_memory_space_constraint(jnp.asarray(x), pltpu.HBM)
        for x in (image, phases, table, start, wg, ws, zg, zs)))


def harmonic(p, q):
    total = p + q
    return 2.0 * p * q / jnp.where(total > 0, total, 1.0)


def step_of(count):
    return max(n for n in (1, 2, 3, 4) if count % n == 0)


def sweep_kernel(cond, start, centre, out, kx, y0, y1, z0, z1, inv, one, two, three,
                 *sems):
    rows, wide, z = cond.shape
    copy = pltpu.make_async_copy(
        cond.at[pl.ds(POT_X, rows - 2 * POT_X), pl.ds(POT_Y, wide - 2 * POT_Y)], centre, sems[0])
    copy.start()
    lane = lax.broadcasted_iota(jnp.int32, (1, wide, z), 2)
    at_low, at_high = lane == 0, lane == z - 1

    def roll_y(v, s):
        return pltpu.roll(v, s % wide, 1)

    def roll_z(v, s):
        return pltpu.roll(v, s % z, 2)

    kx[0] = harmonic(cond[0], cond[1])
    size = 2

    def coefficients(step, carry):
        j = 1 + step * size
        c = cond[pl.ds(j, size)]
        x_up = harmonic(c, cond[pl.ds(j + 1, size)])
        y_up = harmonic(c, roll_y(c, -1))
        z_up = harmonic(c, roll_z(c, -1))
        x_down = jnp.concatenate([kx[j - 1][None], x_up[:size - 1]], axis=0)
        y_down = roll_y(y_up, 1)
        low = jnp.where(at_low, c, roll_z(z_up, 1))
        high = jnp.where(at_high, c, z_up)
        total = x_down + x_up + y_down + y_up + low + high
        kx[pl.ds(j, size)] = x_up
        y0[pl.ds(j, size)] = y_down
        y1[pl.ds(j, size)] = y_up
        z0[pl.ds(j, size)] = low
        z1[pl.ds(j, size)] = jnp.where(at_high, 0.0, z_up)
        inv[pl.ds(j, size)] = 1.0 / jnp.where(total > 0, total, 1.0)
        return carry

    lax.fori_loop(0, (rows - 2) // size, coefficients, 0)

    def relaxed(src, j, size, first, last):
        at, cols = pl.ds(j, size), pl.ds(first, last - first)
        p = src[at]
        own = p[:, first:last]
        if first > 0:
            below, above = p[:, first - 1:last - 1], p[:, first + 1:last + 1]
        else:
            below, above = roll_y(p, 1), roll_y(p, -1)
        numer = kx[pl.ds(j - 1, size), cols] * src[pl.ds(j - 1, size), cols]
        numer = numer + kx[at, cols] * src[pl.ds(j + 1, size), cols]
        numer = numer + y0[at, cols] * below + y1[at, cols] * above
        numer = numer + z0[at, cols] * jnp.where(at_low[:, first:last], 1.0, roll_z(own, 1))
        numer = numer + z1[at, cols] * roll_z(own, -1)
        return numer * inv[at, cols]

    def sweep(src, dst, first, last):
        size = step_of(last - first)

        def step(k, carry):
            j = first + k * size
            dst[pl.ds(j, size)] = relaxed(src, j, size, 0, wide)
            return carry
        lax.fori_loop(0, (last - first) // size, step, 0)

    sweep(start, one, 1, rows - 1)
    sweep(one, two, 2, rows - 2)
    brick = rows - 2 * POT_X
    size = brick // PIECES
    sends = []
    for k in range(PIECES):
        part = pl.ds(k * size, size)
        three[part] = relaxed(two, POT_X + k * size, size, POT_Y, wide - POT_Y)
        sends.append(pltpu.make_async_copy(three.at[part], out.at[part], sems[1 + k]))
        sends[-1].start()
    copy.wait()
    for send in sends:
        send.wait()


def sweeps(cond_ext, pot_ext):
    rows, wide, z = cond_ext.shape
    vmem = pl.BlockSpec(memory_space=pltpu.VMEM)
    brick = jax.ShapeDtypeStruct((rows - 2 * POT_X, wide - 2 * POT_Y, z), F32)
    return pl.pallas_call(
        sweep_kernel,
        out_shape=[brick, brick],
        in_specs=[vmem] * 2,
        out_specs=[pl.BlockSpec(memory_space=pl.ANY)] * 2,
        scratch_shapes=[pltpu.VMEM((rows, wide, z), F32)] * 8 + [
            pltpu.VMEM(brick.shape, F32)] + [pltpu.SemaphoreType.DMA] * (1 + PIECES),
        compiler_params=pltpu.CompilerParams(vmem_limit_bytes=VMEM_LIMIT),
    )(cond_ext, pot_ext)


def body(image, phases, phase_table, start_potential):
    cond_ext, pot_ext = tensor(image, phases, phase_table, start_potential)
    conductivity, potential = sweeps(cond_ext, pot_ext)
    return conductivity, potential


def solution(mesh):
    placed = (P("gx", "gy", None), P("gx", "gy", None), P(), P("gx", "gy", None))
    return jax.shard_map(
        body,
        mesh=mesh,
        in_specs=placed,
        out_specs=(P("gx", "gy", None), P("gx", "gy", None)),
        check_vma=False,
    )
```
